32 devices in a mesh: wide: 16 (over z, x, core), narrow: 2 (over y).
Axes of the slice: x: 2, y: 2, z: 4, core: 2. Of those that a mesh axis runs over, the one named last changes fastest.
Arguments:
- patch_input: bfloat16 [32, 2048, 768], P('wide', 'narrow'), may hold values from -6 to 6
- text_input: bfloat16 [32, 1024, 768], P('wide', 'narrow'), may hold values from -6 to 6
- patch_cotangent: bfloat16 [32, 2048, 768], P('wide', 'narrow'), may hold values from -6 to 6
- text_cotangent: bfloat16 [32, 1024, 768], P('wide', 'narrow'), may hold values from -6 to 6
- patch_count: int32 [32], P('wide'), may hold values from 1024 to 2048, as said below
- header_len: int32 [32], P('wide'), may hold values from 128 to 512, as said below
- text_len: int32 [32], P('wide'), may hold values from 256 to 1024, as said below
- norm_gains: bfloat16 [768, 6], P('wide'), may hold values from 0.25 to 1.75
- header_embed: bfloat16 [768], P('wide'), may hold values from -3 to 3
- enc_project: bfloat16 [768, 2304], P('wide'), may hold values from -0.21875 to 0.21875
- enc_output: bfloat16 [768, 768], P('wide'), may hold values from -6 to 6
- enc_gate_up: bfloat16 [768, 4096], P('wide'), may hold values from -0.21875 to 0.21875
- enc_down: bfloat16 [2048, 768], P('wide'), may hold values from -0.25 to 0.25
- self_project: bfloat16 [768, 2304], P('wide'), may hold values from -0.21875 to 0.21875
- self_output: bfloat16 [768, 768], P('wide'), may hold values from -1.5 to 1.5
- cross_project: bfloat16 [768, 2304], P('wide'), may hold values from -0.21875 to 0.21875
- cross_output: bfloat16 [768, 768], P('wide'), may hold values from -6 to 6
- dec_gate_up: bfloat16 [768, 4096], P('wide'), may hold values from -0.21875 to 0.21875
- dec_down: bfloat16 [2048, 768], P('wide'), may hold values from -0.25 to 0.25
Outputs:
- patch_output: bfloat16 [32, 2048, 768], P('wide', 'narrow')
- text_output: bfloat16 [32, 1024, 768], P('wide', 'narrow')
- patch_input_grad: float32 [32, 2048, 768], P('wide', 'narrow')
- text_input_grad: float32 [32, 1024, 768], P('wide', 'narrow')
- norm_gains_grad: float32 [768, 6], P('wide')
- header_embed_grad: float32 [768], P('wide')
- enc_project_grad: float32 [768, 2304], P('wide')
- enc_output_grad: float32 [768, 768], P('wide')
- enc_gate_up_grad: float32 [768, 4096], P('wide')
- enc_down_grad: float32 [2048, 768], P('wide')
- self_project_grad: float32 [768, 2304], P('wide')
- self_output_grad: float32 [768, 768], P('wide')
- cross_project_grad: float32 [768, 2304], P('wide')
- cross_output_grad: float32 [768, 768], P('wide')
- dec_gate_up_grad: float32 [768, 4096], P('wide')
- dec_down_grad: float32 [2048, 768], P('wide')
The draws below stay inside these ranges and needn't reach their ends.
Inputs may be any that keep to these rules, and one draw needn't show every extreme that they name: `patch_count`: in each aligned group of 2 items, one item has all 2048 patches; rows at or past an item's count are padding. `header_len`: less than the item's patch_count. `text_len`: in each aligned group of 2 items, one item has all 1024 tokens.
All inputs are finite; a program needn't handle non-finite values.
Results may differ from the reference program's by a relative error of at most 0.022.
Values may be sent and summed in bfloat16 or wider, within the bound.
No kernel may reach another device: no remote copies, remote signals or barrier semaphores. Data moves between devices by JAX's collectives and lax.ppermute only.
A program may use at most 280 MiB of HBM per device.

```python
import math
import jax
import jax.numpy as jnp
from jax import lax

D = 768
HEADS = 12
HEAD_DIM = 64
FF = 2048
ITEM_DEV = 2
ITEMS = 32
PATCHES = 2048
TEXT = 1024


def full_slots(key, salt):
    picked = jax.random.randint(jax.random.fold_in(key, salt), (ITEMS // ITEM_DEV,), 0, ITEM_DEV)
    return jnp.arange(ITEM_DEV)[None, :] == picked[:, None]


def draw_patch_count(key, part):
    chosen = full_slots(key, 101)
    key = jax.random.fold_in(key, 1)
    drawn = jax.random.randint(key, (ITEMS // ITEM_DEV, ITEM_DEV), PATCHES // 2, PATCHES + 1)
    return jnp.where(chosen, PATCHES, drawn).reshape(ITEMS).astype(jnp.int32)


def draw_header_len(key, part):
    chosen = full_slots(key, 101)
    key = jax.random.fold_in(key, 2)
    drawn = jax.random.randint(key, (ITEMS // ITEM_DEV, ITEM_DEV), max(1, PATCHES // 16), PATCHES // 4 + 1)
    return jnp.where(chosen, PATCHES // 4, drawn).reshape(ITEMS).astype(jnp.int32)


def draw_text_len(key, part):
    chosen = full_slots(key, 202)
    key = jax.random.fold_in(key, 3)
    drawn = jax.random.randint(key, (ITEMS // ITEM_DEV, ITEM_DEV), TEXT // 4, TEXT + 1)
    return jnp.where(chosen, TEXT, drawn).reshape(ITEMS).astype(jnp.int32)


def level_of(own_key, shape, split, smallest, top_value):
    def one(position, parts):
        steps = jax.random.uniform(jax.random.fold_in(jax.random.fold_in(own_key, 6), position), (parts,), jnp.float32, smallest / len(split), top_value / len(split))
        return jnp.repeat(jnp.exp(steps), shape[position] // parts).reshape((-1,) + (1,) * (len(shape) - position - 1))

    level = one(*split[0])
    for cut in split[1:]:
        level = level * one(*cut)
    return level


def gaussian(stream_key, dims, scale, reach, pieces=(), held_as=jnp.bfloat16):
    entries = jax.random.normal(stream_key, dims, jnp.float32) * scale
    if len(pieces) > 0:
        entries = level_of(stream_key, dims, pieces, -0.22, 0.18) * entries
    return jnp.clip(entries, min=-reach, max=reach).astype(held_as)


def setup_inputs(seed: int = 0) -> dict:
    seeds = jax.random.split(jax.random.key(seed), 20)
    return {
        "patch_input": gaussian(seeds[0], (ITEMS, PATCHES, D), 1.0, 6.0, ((0, 16), (1, 2))),
        "text_input": gaussian(seeds[1], (ITEMS, TEXT, D), 1.0, 6.0, ((0, 16), (1, 2))),
        "patch_cotangent": gaussian(seeds[2], (ITEMS, PATCHES, D), 1.0, 6.0, ((0, 16), (1, 2))),
        "text_cotangent": gaussian(seeds[3], (ITEMS, TEXT, D), 1.0, 6.0, ((0, 16), (1, 2))),
        "patch_count": draw_patch_count(jax.random.fold_in(seeds[19], 71), 0),
        "header_len": draw_header_len(jax.random.fold_in(seeds[19], 71), 0),
        "text_len": draw_text_len(jax.random.fold_in(seeds[19], 71), 0),
        "norm_gains": jnp.clip(1.0 + 0.15 * jax.random.normal(seeds[7], (D, 6), jnp.float32), 0.25, 1.75).astype(jnp.bfloat16),
        "header_embed": gaussian(seeds[8], (D,), 0.5, 3.0, ((0, 16),)),
        "enc_project": gaussian(seeds[9], (D, 3 * D), D ** -0.5, 0.21875, ((0, 16),)),
        "enc_output": gaussian(seeds[10], (D, D), 1 ** -0.5, 6.0, ((0, 16),)),
        "enc_gate_up": gaussian(seeds[11], (D, 2 * FF), D ** -0.5, 0.21875, ((0, 16),)),
        "enc_down": gaussian(seeds[12], (FF, D), (FF // 4) ** -0.5, 0.25, ((0, 16),)),
        "self_project": gaussian(seeds[13], (D, 3 * D), D ** -0.5, 0.21875, ((0, 16),)),
        "self_output": gaussian(seeds[14], (D, D), 16 ** -0.5, 1.5, ((0, 16),)),
        "cross_project": gaussian(seeds[15], (D, 3 * D), D ** -0.5, 0.21875, ((0, 16),)),
        "cross_output": gaussian(seeds[16], (D, D), 1 ** -0.5, 6.0, ((0, 16),)),
        "dec_gate_up": gaussian(seeds[17], (D, 2 * FF), D ** -0.5, 0.21875, ((0, 16),)),
        "dec_down": gaussian(seeds[18], (FF, D), (FF // 4) ** -0.5, 0.25, ((0, 16),)),
    }


@jax.custom_vjp
def low(v):
    return lax.optimization_barrier(v.astype(jnp.bfloat16)).astype(jnp.float32)

@jax.custom_vjp
def low_back(v):
    return v

def low_keep(v):
    return (low(v), None)

def low_pass(kept, grad):
    return (grad,)

def back_keep(v):
    return (v, None)

def back_low(kept, grad):
    return (low(grad),)
low.defvjp(low_keep, low_pass)
low_back.defvjp(back_keep, back_low)
EPSILON = 1e-06
NEGATIVE = -1e+30

def rms_norm(values, gain_row):
    inverse = lax.rsqrt(lax.optimization_barrier(jnp.mean(values * values, axis=-1, keepdims=True)) + EPSILON)
    return values * inverse * gain_row

def dense(left_side, right_side):
    return jnp.dot(left_side, right_side, precision=lax.Precision.HIGHEST)

def gated_gelu(gate_values):
    return jax.nn.gelu(gate_values[:, :FF], approximate=True) * gate_values[:, FF:]

def to_float(array_in):
    return array_in.astype(jnp.float32)

def attention(queries, keys_in, values_in, key_limit, causal):
    query_total = queries.shape[0]
    key_total = keys_in.shape[0]
    block_rows = math.gcd(query_total, 512)
    head_keys = keys_in.reshape(key_total, HEADS, HEAD_DIM)
    head_values = values_in.reshape(key_total, HEADS, HEAD_DIM)
    blocked = queries.reshape(query_total // block_rows, block_rows, HEADS, HEAD_DIM)
    key_pos = jnp.arange(key_total, dtype=jnp.int32)

    def one_block(inputs):
        block_queries, block_index = inputs
        raw_scores = low_back(jnp.einsum('qhd,khd->hqk', block_queries, head_keys, precision=lax.Precision.HIGHEST))
        scores = raw_scores * HEAD_DIM ** (-0.5)
        query_pos = block_index * block_rows + jnp.arange(block_rows, dtype=jnp.int32)
        allowed = jnp.broadcast_to(key_pos[None, :] < key_limit, (block_rows, key_total))
        if causal:
            allowed = jnp.logical_and(allowed, key_pos[None, :] <= query_pos[:, None])
        scores = jnp.where(allowed[None], scores, NEGATIVE)
        row_max = lax.optimization_barrier(jnp.max(scores, axis=-1, keepdims=True))
        exponent = jnp.exp(scores - row_max)
        weights = low(exponent / lax.optimization_barrier(jnp.sum(exponent, axis=-1, keepdims=True)))
        mixed = jnp.einsum('hqk,khd->qhd', weights, head_values, precision=lax.Precision.HIGHEST)
        return mixed.reshape(block_rows, D)
    index_list = jnp.arange(query_total // block_rows, dtype=jnp.int32)
    blocks_out = lax.map(jax.checkpoint(one_block), (blocked, index_list))
    return blocks_out.reshape(query_total, D)

def reference(patch_input, text_input, patch_cotangent, text_cotangent, patch_count, header_len, text_len, norm_gains, header_embed, enc_project, enc_output, enc_gate_up, enc_down, self_project, self_output, cross_project, cross_output, dec_gate_up, dec_down):
    floats = tuple(map(to_float, (patch_input, text_input, norm_gains, header_embed, enc_project, enc_output, enc_gate_up, enc_down, self_project, self_output, cross_project, cross_output, dec_gate_up, dec_down)))

    def forward_all(arrays):
        patches, texts, gain_table, header_row, enc_project, enc_output, enc_gate_up, enc_down, self_project, self_output, cross_project, cross_output, dec_gate_up, dec_down = arrays

        def one_item(inputs):
            patch_rows, text_rows_in, patch_total, header_count, text_total = inputs
            header_mask = (jnp.arange(PATCHES, dtype=jnp.int32) < header_count).astype(jnp.float32)
            patch_start = patch_rows + header_mask[:, None] * header_row
            attn_input = low(rms_norm(patch_start, gain_table[:, 0]))
            enc_qkv = low(low_back(dense(attn_input, enc_project)))
            enc_attended = low(low_back(attention(enc_qkv[:, :D], enc_qkv[:, D:2 * D], enc_qkv[:, 2 * D:], patch_total, False)))
            patch_middle = patch_start + low_back(dense(enc_attended, enc_output))
            mlp_input = low(rms_norm(patch_middle, gain_table[:, 1]))
            enc_gate_values = low_back(dense(mlp_input, enc_gate_up))
            enc_hidden = low(gated_gelu(enc_gate_values))
            patch_final = patch_middle + low_back(dense(enc_hidden, enc_down))
            self_input = low(rms_norm(text_rows_in, gain_table[:, 2]))
            self_qkv = low(low_back(dense(self_input, self_project)))
            self_attended = low(low_back(attention(self_qkv[:, :D], self_qkv[:, D:2 * D], self_qkv[:, 2 * D:], text_total, True)))
            text_middle = text_rows_in + low_back(dense(self_attended, self_output))
            cross_input = low(rms_norm(text_middle, gain_table[:, 3]))
            memory_input = low(rms_norm(patch_final, gain_table[:, 4]))
            cross_queries = low(low_back(dense(cross_input, cross_project[:, :D])))
            memory_kv = low(low_back(dense(memory_input, cross_project[:, D:])))
            cross_attended = low(low_back(attention(cross_queries, memory_kv[:, :D], memory_kv[:, D:], patch_total, False)))
            text_late = text_middle + low_back(dense(cross_attended, cross_output))
            ffn_input = low(rms_norm(text_late, gain_table[:, 5]))
            ffn_gate_values = low_back(dense(ffn_input, dec_gate_up))
            ffn_hidden = low(gated_gelu(ffn_gate_values))
            text_final = text_late + low_back(dense(ffn_hidden, dec_down))
            return (patch_final, text_final)
        return lax.map(jax.checkpoint(one_item), (patches, texts, patch_count, header_len, text_len))
    outputs, pullback = jax.vjp(forward_all, floats)
    grads = pullback((patch_cotangent.astype(jnp.float32), text_cotangent.astype(jnp.float32)))[0]
    return (outputs[0].astype(jnp.bfloat16), outputs[1].astype(jnp.bfloat16), grads[0], grads[1], grads[2], grads[3], grads[4], grads[5], grads[6], grads[7], grads[8], grads[9], grads[10], grads[11], grads[12], grads[13])
```

```python
import functools
import math

import jax
import jax.numpy as jnp
from jax import lax
from jax.experimental import pallas as pl
from jax.experimental.pallas import tpu as pltpu
from jax.sharding import PartitionSpec as P

D = 768
HEADS = 12
HEAD_DIM = 64
FF = 2048
PAIR = 2 * HEAD_DIM
PAIRS = HEADS // 2
FF_BLOCK = 256
GELU_SCALE = 0.7978845608028654
GELU_CUBE = 0.044715


EPSILON = 1e-06
NEGATIVE = -1e30
BF16 = jnp.bfloat16
F32 = jnp.float32


def rms_scale(values):
    return lax.rsqrt(jnp.mean(values * values, axis=-1, keepdims=True) + EPSILON)


def rms_norm(values, gain_row):
    inverse = rms_scale(values)
    return (values * inverse * gain_row).astype(BF16)


def matmul(left_side, right_side):
    return jnp.dot(left_side, right_side, preferred_element_type=F32)


def matmul_back(left_side, right_side):
    return lax.dot_general(
        left_side, right_side, (((1,), (1,)), ((), ())), preferred_element_type=F32
    )


def dot(left_side, right_side):
    return jnp.dot(left_side, right_side, preferred_element_type=F32)


def lanes_of(rows):
    return lax.broadcasted_iota(jnp.int32, (rows, PAIR), 1)


def place(lane, first_lane, columns):
    filled = jnp.zeros(lane.shape, F32)
    for offset, column in enumerate(columns):
        filled = jnp.where(lane == first_lane + offset, column, filled)
    return filled


def three_parts(values):
    high = values.astype(BF16).astype(F32)
    rest = values - high
    middle = rest.astype(BF16).astype(F32)
    return (high, middle, (rest - middle).astype(BF16).astype(F32))


def both_heads(lane, pair_values, columns):
    first = jnp.where(lane < HEAD_DIM, pair_values, place(lane, HEAD_DIM, columns))
    second = jnp.where(lane >= HEAD_DIM, pair_values, place(lane, 0, columns))
    return (first.astype(BF16), second.astype(BF16))


def key_bias(first_key, rows, limit):
    position = first_key + lax.broadcasted_iota(jnp.int32, (rows, PAIR), 0)
    return jnp.where(position < limit, 0.0, NEGATIVE)


def forward_kernel(
    causal,
    aligned,
    scalars_ref,
    query_ref,
    key_ref,
    value_ref,
    out_ref,
    exact_ref,
    total_ref,
    key_first,
    key_second,
    value_first,
    value_second,
    key_bound,
):
    item = pl.program_id(0)
    block = pl.program_id(2)
    block_rows = query_ref.shape[1]
    key_total = key_ref.shape[1]
    limit = scalars_ref[1 + item]
    query_start = scalars_ref[0]

    def longest(lane, pair_values):
        square = pair_values * pair_values
        first = jnp.sum(jnp.where(lane < HEAD_DIM, square, 0.0), axis=1, keepdims=True)
        second = jnp.sum(jnp.where(lane >= HEAD_DIM, square, 0.0), axis=1, keepdims=True)
        return (jnp.max(first), jnp.max(second))

    @pl.when(block == 0)
    def prepare():
        lane = lanes_of(key_total)
        pair_keys = key_ref[0].astype(F32)
        keys = both_heads(lane, pair_keys, (key_bias(0, key_total, limit),))
        key_first[...] = keys[0].T
        key_second[...] = keys[1].T
        values = value_ref[0].astype(F32)
        value_first[...] = jnp.where(lane < HEAD_DIM, values, 1.0).astype(BF16)
        value_second[...] = jnp.where(lane >= HEAD_DIM, values, 1.0).astype(BF16)
        bounds = longest(lane, pair_keys)
        key_bound[0] = bounds[0]
        key_bound[1] = bounds[1]

    lane = lanes_of(block_rows)
    own = lane < HEAD_DIM
    scaled = query_ref[0].astype(F32) * HEAD_DIM ** (-0.5)
    queries = both_heads(lane, scaled, (1.0,))
    bounds = longest(lane, scaled)
    bound = jnp.maximum(bounds[0] * key_bound[0], bounds[1] * key_bound[1])
    sides = ((queries[0], key_first, value_first), (queries[1], key_second, value_second))

    def score_piece(head_queries, head_keys, piece):
        first_key, width, masked = piece
        scores = dot(head_queries, head_keys[:, first_key : first_key + width])
        if masked:
            row_pos = (
                query_start
                + block * block_rows
                + lax.broadcasted_iota(jnp.int32, (block_rows, width), 0)
            )
            key_pos = first_key + lax.broadcasted_iota(jnp.int32, (block_rows, width), 1)
            scores = jnp.where(key_pos <= row_pos, scores, NEGATIVE)
        return scores

    def store(sums, shifts):
        row_sum = pltpu.roll(jnp.where(own, sums[1], sums[0]), HEAD_DIM, 1)
        exact = jnp.where(own, sums[0], sums[1]) / row_sum
        exact_ref[0] = exact
        out_ref[0] = exact.astype(BF16)
        total_ref[0] = jnp.where(own, shifts[0], shifts[1]) + jnp.log(row_sum)

    def unshifted(pieces):
        units = [(piece, side) for piece in pieces for side in range(2)]

        def scores_of(unit):
            piece, side = unit
            return score_piece(sides[side][0], sides[side][1], piece)

        sums = [None, None]
        ahead = scores_of(units[0])
        for index, (piece, side) in enumerate(units):
            scores = ahead
            if index + 1 < len(units):
                ahead = scores_of(units[index + 1])
            weights = jnp.exp(scores).astype(BF16)
            term = dot(weights, sides[side][2][piece[0] : piece[0] + piece[1], :])
            sums[side] = term if sums[side] is None else sums[side] + term
        store(sums, (0.0, 0.0))

    def shifted(pieces):
        sums = []
        shifts = []
        for head_queries, head_keys, head_values in sides:
            scores = [score_piece(head_queries, head_keys, piece) for piece in pieces]
            row_max = None
            for part in scores:
                part_max = jnp.max(part, axis=1, keepdims=True)
                row_max = part_max if row_max is None else jnp.maximum(row_max, part_max)
            summed = None
            for piece, part in zip(pieces, scores):
                weights = jnp.exp(part - row_max).astype(BF16)
                term = dot(weights, head_values[piece[0] : piece[0] + piece[1], :])
                summed = term if summed is None else summed + term
            sums.append(summed)
            shifts.append(row_max)
        store(sums, shifts)

    def run(pieces):
        @pl.when(bound <= 1600.0)
        def plain():
            unshifted(pieces)

        @pl.when(bound > 1600.0)
        def general():
            shifted(pieces)

    def whole_row(masked):
        step = min(512, key_total)
        return [(first, step, masked) for first in range(0, key_total, step)]

    if not causal:
        run(whole_row(False))
    elif not aligned:
        run(whole_row(True))
    else:
        for index in range(key_total // block_rows):

            @pl.when(block == index)
            def one_block(index=index):
                first_key = index * block_rows
                pieces = [(0, first_key, False)] if index else []
                run(pieces + [(first_key, block_rows, True)])


def backward_kernel(
    causal,
    aligned,
    chunk_rows,
    scalars_ref,
    query_ref,
    key_ref,
    value_ref,
    grad_ref,
    exact_ref,
    total_ref,
    *refs,
):
    if len(refs) == 9:
        query_grad_ref, key_grad_ref = refs[:2]
        key_at = 0
    else:
        query_grad_ref = key_grad_ref = refs[0]
        key_at = PAIR
    (
        query_first,
        query_second,
        grad_first,
        grad_second,
        query_across,
        grad_across,
        query_sum,
    ) = refs[-7:]
    item = pl.program_id(0)
    block = pl.program_id(2)
    query_total = query_ref.shape[1]
    block_keys = key_ref.shape[1]
    limit = scalars_ref[1 + item]
    query_start = scalars_ref[0]
    scale = HEAD_DIM ** (-0.5)

    @pl.when(block == 0)
    def prepare():
        lane = lanes_of(query_total)
        own = lane < HEAD_DIM
        scaled = query_ref[0].astype(F32) * scale
        query_across[...] = scaled.astype(BF16).T
        total = -pltpu.roll(total_ref[0], HEAD_DIM, 1)
        queries = both_heads(lane, scaled, (1.0,) + three_parts(total))
        query_first[...] = queries[0]
        query_second[...] = queries[1]
        grads = grad_ref[0].astype(F32)
        grad_across[...] = grad_ref[0].T
        product = grads * exact_ref[0]
        first_sum = jnp.sum(jnp.where(own, product, 0.0), axis=1, keepdims=True)
        second_sum = jnp.sum(jnp.where(own, 0.0, product), axis=1, keepdims=True)
        weighted = -jnp.where(own, second_sum, first_sum)
        head_grads = both_heads(lane, grads, three_parts(weighted))
        grad_first[...] = head_grads[0]
        grad_second[...] = head_grads[1]
        query_sum[...] = jnp.zeros_like(query_sum)

    lane = lanes_of(block_keys)
    bias = key_bias(block * block_keys, block_keys, limit)
    pair_keys = key_ref[0].astype(F32)
    keys = [part.T for part in both_heads(lane, pair_keys, (bias, 1.0, 1.0, 1.0))]
    values = [
        part.T for part in both_heads(lane, value_ref[0].astype(F32), (1.0, 1.0, 1.0))
    ]
    keys_across = (pair_keys * scale).astype(BF16).T

    def run(pieces):
        key_parts = [None, None]
        value_parts = [None, None]
        units = [(piece, head) for piece in pieces for head in range(2)]
        sides = ((query_first, grad_first), (query_second, grad_second))

        def products_of(unit):
            (first_row, width, masked), head = unit
            rows = slice(first_row, first_row + width)
            scores = dot(sides[head][0][rows, :], keys[head])
            if masked:
                row_pos = (
                    query_start
                    + first_row
                    + lax.broadcasted_iota(jnp.int32, (width, block_keys), 0)
                )
                key_pos = block * block_keys + lax.broadcasted_iota(
                    jnp.int32, (width, block_keys), 1
                )
                scores = jnp.where(key_pos <= row_pos, scores, NEGATIVE)
            return (scores, dot(sides[head][1][rows, :], values[head]))

        ahead = products_of(units[0])
        for index, ((first_row, width, masked), head) in enumerate(units):
            scores, weight_grad = ahead
            if index + 1 < len(units):
                ahead = products_of(units[index + 1])
            rows = slice(first_row, first_row + width)
            head_rows = slice(head * HEAD_DIM, (head + 1) * HEAD_DIM)
            weights = jnp.exp(scores)
            score_grad = (weights * weight_grad).astype(BF16)
            value_term = dot(grad_across[head_rows, rows], weights.astype(BF16))
            key_term = dot(query_across[head_rows, rows], score_grad)
            query_sum[head_rows, rows] += matmul_back(keys_across[head_rows, :], score_grad)
            if key_parts[head] is None:
                key_parts[head], value_parts[head] = key_term, value_term
            else:
                key_parts[head] = key_parts[head] + key_term
                value_parts[head] = value_parts[head] + value_term
        block_rows = pl.ds(pl.multiple_of(block * block_keys, block_keys), block_keys)
        key_grad_ref[0, block_rows, key_at : key_at + PAIR] = (
            jnp.concatenate(key_parts, axis=0).T.astype(BF16)
        )
        key_grad_ref[0, block_rows, key_at + PAIR : key_at + 2 * PAIR] = (
            jnp.concatenate(value_parts, axis=0).T.astype(BF16)
        )

    def chunks(first_row, masked):
        return [
            (start, min(chunk_rows, query_total - start), masked)
            for start in range(first_row, query_total, chunk_rows)
        ]

    if not causal:
        run(chunks(0, False))
    elif not aligned:
        run(chunks(0, True))
    else:
        for index in range(query_total // block_keys):

            @pl.when(block == index)
            def one_block(index=index):
                first_row = index * block_keys
                run(
                    [(first_row, block_keys, True)]
                    + chunks(first_row + block_keys, False)
                )

    @pl.when(block == pl.num_programs(2) - 1)
    def finish():
        query_grad_ref[0, :, :PAIR] = query_sum[...].T.astype(BF16)


VMEM_BYTES = 56 * 1024 * 1024
SMALL_COST = pl.CostEstimate(flops=1000, bytes_accessed=1000, transcendentals=0)


def row_scale(values):
    return lax.rsqrt(jnp.mean(values * values, axis=1, keepdims=True) + EPSILON)


def norm_back(gradient, values, gain):
    inverse = row_scale(values)
    unit = values * inverse
    gain_grad = jnp.sum(gradient * unit, axis=0, keepdims=True)
    scaled = gradient * gain
    inner_mean = jnp.mean(scaled * unit, axis=1, keepdims=True)
    return (inverse * (scaled - unit * inner_mean), gain_grad)


def add_rows(total_ref, row):
    @pl.when(pl.program_id(0) == 0)
    def start():
        total_ref[...] = jnp.zeros_like(total_ref)

    total_ref[0:1, :] += row


def unpack_down(packed_ref, down_ref):
    for device in range(16):
        for group in range(8):
            for column in range(D // 256):
                row = (device * 8 + group) * 16
                down_ref[row : row + 16, column * 256 : (column + 1) * 256] = packed_ref[
                    device * 48 + column * 16 : device * 48 + (column + 1) * 16,
                    group * 256 : (group + 1) * 256,
                ]


def layer_forward_kernel(
    gain_row,
    next_row,
    attended_ref,
    start_ref,
    gate_up_ref,
    packed_ref,
    output_ref,
    gains_ref,
    middle_ref,
    normed_ref,
    slopes_ref,
    hidden_ref,
    rounded_ref,
    *refs,
):
    rows_ref, down_ref = refs[-2:]

    @pl.when(pl.program_id(0) == 0)
    def unpack():
        unpack_down(packed_ref, down_ref)

    middle = start_ref[...].astype(F32) + dot(attended_ref[...], output_ref[...])
    middle_ref[...] = middle
    normed = (middle * row_scale(middle) * gains_ref[gain_row : gain_row + 1, :]).astype(BF16)
    normed_ref[...] = normed.T

    span = 2 * FF_BLOCK

    def product_of(first):
        return dot(normed, gate_up_ref[:, 2 * first : 2 * (first + span)])

    ahead = product_of(0)
    for start in range(0, FF, span):
        product = ahead
        if start + span < FF:
            ahead = product_of(start + span)
        for first in range(start, start + span, FF_BLOCK):
            both = product[:, 2 * (first - start) : 2 * (first - start + FF_BLOCK)]
            gate, up = both[:, :FF_BLOCK], both[:, FF_BLOCK:]
            square = gate * gate
            bend = jnp.tanh(gate * (GELU_SCALE + (GELU_SCALE * GELU_CUBE) * square))
            half = 0.5 + 0.5 * bend
            bent = gate * half
            slope = half + (1.0 - bend * bend) * (
                gate * (0.5 * GELU_SCALE + (1.5 * GELU_SCALE * GELU_CUBE) * square)
            )
            slopes_ref[:, 2 * first : 2 * first + FF_BLOCK] = (up * slope).astype(BF16)
            slopes_ref[:, 2 * first + FF_BLOCK : 2 * (first + FF_BLOCK)] = bent.astype(BF16)
            hidden = (bent * up).astype(BF16)
            rows_ref[:, first : first + FF_BLOCK] = hidden
            hidden_ref[first : first + FF_BLOCK, :] = hidden.T
    final = middle + dot(rows_ref[...], down_ref[...])
    rounded_ref[...] = final.astype(BF16)
    if next_row is not None:
        refs[0][...] = final
        next_normed = (
            final * row_scale(final) * gains_ref[next_row : next_row + 1, :]
        ).astype(BF16)
        refs[1][...] = next_normed
        refs[2][...] = next_normed.T


def layer_backward_kernel(
    gain_row,
    grad_ref,
    slopes_ref,
    middle_ref,
    gate_up_ref,
    packed_ref,
    output_ref,
    gains_ref,
    gate_grad_ref,
    middle_grad_ref,
    rounded_ref,
    head_grad_ref,
    gain_grad_ref,
    down_ref,
):
    @pl.when(pl.program_id(0) == 0)
    def unpack():
        unpack_down(packed_ref, down_ref)

    out_grad = grad_ref[...].astype(BF16)

    span = 2 * FF_BLOCK

    def product_of(first):
        return matmul_back(out_grad, down_ref[first : first + span, :])

    ahead = product_of(0)
    for start in range(0, FF, span):
        product = ahead
        if start + span < FF:
            ahead = product_of(start + span)
        for first in range(start, start + span, FF_BLOCK):
            both = slice(2 * first, 2 * (first + FF_BLOCK))
            hidden_grad = product[:, first - start : first - start + FF_BLOCK]
            hidden_grad = jnp.concatenate([hidden_grad, hidden_grad], axis=1)
            gate_grad_ref[:, both] = (hidden_grad * slopes_ref[:, both].astype(F32)).astype(BF16)
    normed_grad = matmul_back(gate_grad_ref[...], gate_up_ref[...])
    in_grad, gain_grad = norm_back(
        normed_grad, middle_ref[...], gains_ref[gain_row : gain_row + 1, :]
    )
    add_rows(gain_grad_ref, gain_grad)
    middle_grad = grad_ref[...].astype(F32) + in_grad
    middle_grad_ref[...] = middle_grad
    rounded = middle_grad.astype(BF16)
    rounded_ref[...] = rounded
    head_grad_ref[...] = matmul_back(rounded, output_ref[...]).astype(BF16)


def project_back_kernel(gain_row, sides, with_rounded, with_head, *refs):
    grads, weights = refs[:sides], refs[sides : 2 * sides]
    base_ref, values_ref, gains_ref = refs[2 * sides : 2 * sides + 3]
    outs = list(refs[2 * sides + 3 :])
    output_ref = outs.pop(0) if with_head else None
    normed_grad = None
    for grad_ref, weight_ref in zip(grads, weights):
        term = matmul_back(grad_ref[...], weight_ref[...])
        normed_grad = term if normed_grad is None else normed_grad + term
    in_grad, gain_grad = norm_back(
        normed_grad, values_ref[...].astype(F32), gains_ref[gain_row : gain_row + 1, :]
    )
    total = base_ref[...].astype(F32) + in_grad
    outs[0][...] = total
    add_rows(outs[1], gain_grad)
    if with_rounded:
        rounded = total.astype(BF16)
        outs[2][...] = rounded
        if with_head:
            outs[3][...] = matmul_back(rounded, output_ref[...]).astype(BF16)


def rows_call(kernel, rows, operands, outs, scratch, name):
    step = min(512, rows)
    in_specs = []
    for array, stays in operands:
        if stays is None:
            in_specs.append(pl.BlockSpec((step, array.shape[1]), lambda m: (m, 0)))
        else:
            width, column = stays
            in_specs.append(
                pl.BlockSpec(
                    (array.shape[0], width),
                    functools.partial(lambda at, m: (0, at), column // width),
                    pipeline_mode=pl.Buffered(1),
                )
            )
    out_specs = []
    out_shape = []
    for width, dtype, *across in outs:
        if across:
            out_specs.append(pl.BlockSpec((width, step), lambda m: (0, m)))
            out_shape.append(jax.ShapeDtypeStruct((width, rows), dtype))
        elif dtype is None:
            out_specs.append(pl.BlockSpec((8, width), lambda m: (0, 0)))
            out_shape.append(jax.ShapeDtypeStruct((8, width), F32))
        else:
            out_specs.append(pl.BlockSpec((step, width), lambda m: (m, 0)))
            out_shape.append(jax.ShapeDtypeStruct((rows, width), dtype))
    return pl.pallas_call(
        kernel,
        grid=(rows // step,),
        in_specs=in_specs,
        out_specs=out_specs,
        out_shape=out_shape,
        scratch_shapes=scratch,
        compiler_params=pltpu.CompilerParams(vmem_limit_bytes=VMEM_BYTES),
        cost_estimate=SMALL_COST,
        name=name,
    )(*[array for array, stays in operands])


LAYER_SIDES = ((2 * FF, 0), (FF, 2 * FF), (D, 3 * FF))


def layer_forward(attended, start, layer, gains, gain_row, next_row=None):
    outs = [(D, F32), (D, BF16, True), (2 * FF, BF16), (FF, BF16, True), (D, BF16)]
    if next_row is not None:
        outs += [(D, F32), (D, BF16), (D, BF16, True)]
    return rows_call(
        functools.partial(layer_forward_kernel, gain_row, next_row),
        attended.shape[0],
        [(attended, None), (start, None)]
        + [(layer, side) for side in LAYER_SIDES]
        + [(gains, (D, 0))],
        outs,
        [pltpu.VMEM((min(512, attended.shape[0]), FF), BF16), pltpu.VMEM((FF, D), BF16)],
        "layer_forward",
    )


def layer_backward(grad, slopes, middle, layer, gains, gain_row):
    return rows_call(
        functools.partial(layer_backward_kernel, gain_row),
        grad.shape[0],
        [(grad, None), (slopes, None), (middle, None)]
        + [(layer, side) for side in LAYER_SIDES]
        + [(gains, (D, 0))],
        [(2 * FF, BF16), (D, F32), (D, BF16), (D, BF16), (D, None)],
        [pltpu.VMEM((FF, D), BF16)],
        "layer_backward",
    )


def project_back(sides, base, values, gains, gain_row, rounded=False, output=None):
    operands = [(grad, None) for grad, weight, place in sides]
    operands += [(weight, place) for grad, weight, place in sides]
    operands += [(base, None), (values, None), (gains, (D, 0))]
    outs = [(D, F32), (D, None)]
    if rounded:
        outs.append((D, BF16))
    if output is not None:
        operands.append(output)
        outs.append((D, BF16))
    return rows_call(
        functools.partial(
            project_back_kernel, gain_row, len(sides), rounded, output is not None
        ),
        base.shape[0],
        operands,
        outs,
        [],
        "project_back",
    )


def weight_grad_kernel(left_ref, right_ref, *refs):
    out_ref, across = refs[-2:]

    @pl.when(pl.program_id(0) == 0)
    def turn():
        step = min(256, left_ref.shape[0])
        for first_row in range(0, left_ref.shape[0], step):
            across[:, first_row : first_row + step] = left_ref[first_row : first_row + step, :].T

    out_ref[...] = dot(across[...], right_ref[...]).astype(BF16)


def turned_grad_kernel(left_ref, right_ref, *refs):
    refs[-1][...] = dot(left_ref[...], right_ref[...]).astype(BF16)


def turn_kernel(rows_ref, out_ref):
    out_ref[...] = rows_ref[...].T


def turn_rows(array):
    return rows_call(
        turn_kernel, array.shape[0], [(array, None)], [(array.shape[1], BF16, True)], [], "turn_rows"
    )[0]


def down_grad_kernel(shard_rows, hidden_ref, right_ref, *refs):
    out_ref = refs[-1]
    term = dot(hidden_ref[...], right_ref[...]).astype(BF16)
    group_rows = FF * shard_rows // D // 8
    for device in range(out_ref.shape[0] // shard_rows):
        for column in range(D // 256):
            for group in range(8):
                first_row = (device * 8 + group) * group_rows
                out_row = device * shard_rows + column * group_rows
                out_ref[out_row : out_row + group_rows, group * 256 : (group + 1) * 256] = term[
                    first_row : first_row + group_rows, column * 256 : (column + 1) * 256
                ]


def fill_call(kernel, grid, in_specs, out_spec, columns, scratch, operands, buffer, name):
    operands = list(operands)
    in_specs = list(in_specs)
    aliases = {}
    if buffer is not None:
        aliases = {len(operands): 0}
        operands.append(buffer)
        in_specs.append(pl.BlockSpec(memory_space=pl.ANY))
    return pl.pallas_call(
        kernel,
        grid=grid,
        in_specs=in_specs,
        out_specs=out_spec,
        out_shape=jax.ShapeDtypeStruct((D, columns), BF16),
        scratch_shapes=scratch,
        input_output_aliases=aliases,
        compiler_params=pltpu.CompilerParams(vmem_limit_bytes=VMEM_BYTES),
        cost_estimate=SMALL_COST,
        name=name,
    )(*operands)


def fill_weight_grad(buffer, columns, first_column, left_side, right_side, turned=False):
    rows = right_side.shape[0]
    step = 1024 if right_side.shape[1] % 1024 == 0 else D
    first_step = first_column // step
    return fill_call(
        turned_grad_kernel if turned else weight_grad_kernel,
        (right_side.shape[1] // step,),
        [
            pl.BlockSpec(left_side.shape, lambda n: (0, 0)),
            pl.BlockSpec((rows, step), lambda n: (0, n)),
        ],
        pl.BlockSpec((D, step), lambda n: (0, first_step + n)),
        columns,
        [] if turned else [pltpu.VMEM((D, rows), BF16)],
        (left_side, right_side),
        buffer,
        "weight_grad",
    )


def fill_down_grad(buffer, columns, first_column, shard_rows, hidden, out_grad):
    rows = out_grad.shape[0]
    wide = D // shard_rows
    if FF // wide // 8 % 16:
        cut = matmul(hidden, out_grad).astype(BF16).reshape(wide, 8, FF // wide // 8, 3, 256)
        cut = cut.transpose(0, 3, 2, 1, 4).reshape(D, FF)
        return lax.dynamic_update_slice(buffer, cut, (0, first_column))
    devices = math.gcd(wide, 4)
    first_step = first_column // FF
    return fill_call(
        functools.partial(down_grad_kernel, shard_rows),
        (wide // devices,),
        [
            pl.BlockSpec((devices * FF // wide, rows), lambda n: (n, 0)),
            pl.BlockSpec((rows, D), lambda n: (0, 0)),
        ],
        pl.BlockSpec((devices * shard_rows, FF), lambda n: (n, first_step)),
        columns,
        [],
        (hidden, out_grad),
        buffer,
        "down_grad",
    )


def attend_forward(query_side, key_side, value_side, scalars, causal, aligned):
    (query_array, query_at), (key_array, key_at), (value_array, value_at) = (
        query_side,
        key_side,
        value_side,
    )
    query_step, key_step = query_array.shape[2] // D, key_array.shape[2] // D
    items, rows = query_array.shape[0], query_array.shape[1]
    keys = key_array.shape[1]
    block_rows = min(512 if causal else 1024, rows)
    return pl.pallas_call(
        functools.partial(forward_kernel, causal, aligned),
        grid=(items, PAIRS, rows // block_rows),
        in_specs=[
            pl.BlockSpec(memory_space=pltpu.SMEM),
            pl.BlockSpec((1, block_rows, PAIR), lambda i, p, b: (i, b, query_at + query_step * p)),
            pl.BlockSpec((1, keys, PAIR), lambda i, p, b: (i, 0, key_at + key_step * p)),
            pl.BlockSpec((1, keys, PAIR), lambda i, p, b: (i, 0, value_at + key_step * p)),
        ],
        out_specs=[
            pl.BlockSpec((1, block_rows, PAIR), lambda i, p, b: (i, b, p)),
            pl.BlockSpec((1, block_rows, PAIR), lambda i, p, b: (i, b, p)),
            pl.BlockSpec((1, block_rows, PAIR), lambda i, p, b: (i, b, p)),
        ],
        out_shape=[
            jax.ShapeDtypeStruct((items, rows, D), BF16),
            jax.ShapeDtypeStruct((items, rows, D), F32),
            jax.ShapeDtypeStruct((items, rows, D), F32),
        ],
        scratch_shapes=[
            pltpu.VMEM((PAIR, keys), BF16),
            pltpu.VMEM((PAIR, keys), BF16),
            pltpu.VMEM((keys, PAIR), BF16),
            pltpu.VMEM((keys, PAIR), BF16),
            pltpu.SMEM((2,), F32),
        ],
        compiler_params=pltpu.CompilerParams(vmem_limit_bytes=VMEM_BYTES),
        cost_estimate=SMALL_COST,
        name="attend_forward",
    )(scalars, query_array, key_array, value_array)


def attend_backward(
    query_side,
    key_side,
    value_side,
    head_grad,
    exact,
    total,
    scalars,
    causal,
    aligned,
    first_pair=0,
    pairs=PAIRS,
    block_keys=512,
    chunk_rows=1024,
):
    (query_array, query_at), (key_array, key_at), (value_array, value_at) = (
        query_side,
        key_side,
        value_side,
    )
    query_step, key_step = query_array.shape[2] // D, key_array.shape[2] // D
    items, rows = query_array.shape[0], query_array.shape[1]
    keys = key_array.shape[1]
    chunk_rows = min(chunk_rows, rows)
    whole = pl.BlockSpec((1, rows, PAIR), lambda i, p, b: (i, 0, first_pair + p))
    together = query_array is key_array
    if together:
        widths = ((rows, 3 * PAIR),)
    else:
        widths = ((rows, PAIR), (keys, 2 * PAIR))
    return pl.pallas_call(
        functools.partial(backward_kernel, causal, aligned, chunk_rows),
        grid=(items, pairs, keys // block_keys),
        in_specs=[
            pl.BlockSpec(memory_space=pltpu.SMEM),
            pl.BlockSpec((1, rows, PAIR), lambda i, p, b: (i, 0, query_at + query_step * (first_pair + p))),
            pl.BlockSpec((1, block_keys, PAIR), lambda i, p, b: (i, b, key_at + key_step * (first_pair + p))),
            pl.BlockSpec((1, block_keys, PAIR), lambda i, p, b: (i, b, value_at + key_step * (first_pair + p))),
            whole,
            whole,
            whole,
        ],
        out_specs=[pl.BlockSpec((1,) + width, lambda i, p, b: (i, 0, p)) for width in widths],
        out_shape=[
            jax.ShapeDtypeStruct((items, width[0], width[1] * pairs), BF16) for width in widths
        ],
        scratch_shapes=[
            pltpu.VMEM((rows, PAIR), BF16),
            pltpu.VMEM((rows, PAIR), BF16),
            pltpu.VMEM((rows, PAIR), BF16),
            pltpu.VMEM((rows, PAIR), BF16),
            pltpu.VMEM((PAIR, rows), BF16),
            pltpu.VMEM((PAIR, rows), BF16),
            pltpu.VMEM((PAIR, rows), F32),
        ],
        compiler_params=pltpu.CompilerParams(vmem_limit_bytes=VMEM_BYTES),
        cost_estimate=SMALL_COST,
        name="attend_backward",
    )(scalars, query_array, key_array, value_array, head_grad, exact, total)


def in_order(first, second):
    return lax.optimization_barrier((first, second))


def on_device(
    narrow,
    patch_input,
    text_input,
    patch_cotangent,
    text_cotangent,
    patch_count,
    header_len,
    text_len,
    norm_gains,
    header_embed,
    enc_project,
    enc_output,
    enc_gate_up,
    enc_down,
    self_project,
    self_output,
    cross_project,
    cross_output,
    dec_gate_up,
    dec_down,
):
    swapped = narrow == 2 and patch_input.shape[0] == 2
    spot = lax.axis_index("narrow")
    shard_rows = norm_gains.shape[0]
    wide = D // shard_rows

    def partner(array):
        return lax.ppermute(array, "narrow", [(0, 1), (1, 0)])

    def pick(own, got, position):
        slot = jnp.arange(2, dtype=jnp.int32).reshape(2, 1, 1)
        return jnp.where(slot == position, own[None], got[None])

    def take_items(array):
        if not swapped:
            return array
        own = lax.dynamic_index_in_dim(array, spot, 0, keepdims=False)
        got = partner(lax.dynamic_index_in_dim(array, 1 - spot, 0, keepdims=False))
        return pick(own, got, spot).reshape(1, -1, D)

    def halve_rows(array):
        half = array.shape[1] // 2
        own = lax.dynamic_slice_in_dim(array[0], spot * half, half, 0)
        away = lax.dynamic_slice_in_dim(array[0], (1 - spot) * half, half, 0)
        return (own, away.astype(BF16))

    def send_rows(array, tied=None):
        if not swapped:
            return (array, None), tied
        own, away = halve_rows(array)
        away, tied = in_order(away, tied)
        return (own, partner(away)), tied

    def place_rows(sent):
        own, got = sent
        return own if got is None else pick(own, got.astype(own.dtype), spot)

    def gather(*arrays):
        whole = jnp.concatenate(arrays, axis=1) if len(arrays) > 1 else arrays[0]
        return lax.all_gather(whole, "wide", axis=0, tiled=True)

    def scatter(summed):
        return lax.psum_scatter(summed, "wide", scatter_dimension=0, tiled=True)

    def sum_small(array):
        step = 1
        while step < wide:
            ways = min(4, wide // step)
            got = [
                lax.ppermute(
                    array, "wide", [(index, index ^ (step * way)) for index in range(wide)]
                )
                for way in range(1, ways)
            ]
            array = functools.reduce(jnp.add, got, array)
            step *= ways
        return array

    def exchange(summed):
        return partner(summed) if narrow == 2 else None

    def finish(summed, widths, got=None):
        if narrow == 2:
            got = exchange(summed) if got is None else got
            total = summed.astype(F32) + got.astype(F32)
        else:
            total = lax.psum(summed, "narrow").astype(F32)
        parts = []
        start = 0
        for width in widths:
            parts.append(total[:, start : start + width])
            start += width
        return parts

    def gather_layer(gate_up, down, output, *more):
        if FF // wide == 128:
            packed = down.reshape(8, 16, D // 256, 256).transpose(2, 1, 0, 3).reshape(-1, FF)
            return gather(gate_up, packed, output, *more)
        packed = gather(down).reshape(16, 8, 16, D // 256, 256)
        packed = packed.transpose(0, 3, 2, 1, 4).reshape(D, FF)
        return jnp.concatenate([gather(gate_up), packed, gather(output, *more)], axis=1)

    groups = 8
    group_rows = FF // wide // groups

    def rows_to_down(array):
        cut = array.reshape(-1, D // 256, group_rows, groups, 256)
        return cut.transpose(0, 3, 2, 1, 4).reshape(-1, D)

    def by_pair(array):
        sides = array.shape[1] // D
        return array.reshape(-1, sides, PAIRS, PAIR).swapaxes(1, 2).reshape(array.shape)

    def by_side(array):
        sides = array.shape[1] // D
        return array.reshape(-1, PAIRS, sides, PAIR).swapaxes(1, 2).reshape(array.shape)

    def by_block(array):
        return array.reshape(-1, 2, FF // FF_BLOCK, FF_BLOCK).swapaxes(1, 2).reshape(array.shape)

    def by_half(array):
        return array.reshape(-1, FF // FF_BLOCK, 2, FF_BLOCK).swapaxes(1, 2).reshape(array.shape)

    enc_project, self_project = by_pair(enc_project), by_pair(self_project)
    cross_project = jnp.concatenate([cross_project[:, :D], by_pair(cross_project[:, D:])], axis=1)
    enc_gate_up, dec_gate_up = by_block(enc_gate_up), by_block(dec_gate_up)
    small = jnp.concatenate(
        [norm_gains, header_embed[:, None], jnp.zeros((shard_rows, 121), BF16)], axis=1
    )
    patch_rows_in = take_items(patch_input)
    first_group = gather(enc_project, small)
    second_group = gather_layer(enc_gate_up, enc_down, enc_output, self_project)
    third_group = gather(cross_project[:, D:], cross_project[:, :D], self_output)
    small_all = first_group[:, 3 * D :]
    cross_memory_at = (2 * D, 0)
    cross_query_at = (D, 2 * D)
    self_project_at = (3 * D, 3 * FF + D)
    self_output_at = (D, 3 * D)

    def part_of(array, place):
        return array[:, place[1] : place[1] + place[0]]

    items, patch_rows = patch_rows_in.shape[0], patch_rows_in.shape[1]
    text_rows = text_input.shape[1] * (2 if swapped else 1)
    if swapped:
        patch_total = lax.dynamic_slice_in_dim(patch_count, spot, 1)
        header_total = lax.dynamic_slice_in_dim(header_len, spot, 1)
        text_total = lax.dynamic_slice_in_dim(text_len, spot, 1)
        patch_first = jnp.int32(0)
        text_first = jnp.int32(0)
    else:
        patch_total, header_total, text_total = patch_count, header_len, text_len
        patch_first = spot * patch_rows
        text_first = spot * text_rows
    patch_scalars = jnp.concatenate([patch_first[None], patch_total])
    cross_scalars = jnp.concatenate([text_first[None], patch_total])
    text_scalars = jnp.concatenate([text_first[None], text_total])
    patch_flat = items * patch_rows
    text_flat = items * text_rows

    def all_keys(array):
        return array if swapped else lax.all_gather(array, "narrow", axis=1, tiled=True)

    def own_keys(array):
        if swapped:
            return array
        return lax.psum_scatter(array, "narrow", scatter_dimension=1, tiled=True)

    def split_of(projected):
        if swapped:
            return ((projected, 0), (projected, 1), (projected, 2))
        shape = projected.shape[:2]
        by_pair = projected.reshape(shape + (PAIRS, 3 * PAIR))
        keys = all_keys(by_pair[:, :, :, PAIR:].reshape(shape + (2 * D,)))
        return ((by_pair[:, :, :, :PAIR].reshape(shape + (D,)), 0), (keys, 0), (keys, 1))

    def joined(grads):
        if swapped:
            return grads[0].reshape(-1, grads[0].shape[2])
        query_grad, key_grad = grads[0], own_keys(grads[1])
        pairs = query_grad.shape[2] // PAIR
        shape = query_grad.shape[:2] + (pairs, -1)
        return jnp.concatenate(
            [query_grad.reshape(shape), key_grad.reshape(shape)], axis=3
        ).reshape(-1, 3 * pairs * PAIR)

    gains = small_all[:, :8].astype(F32).T
    header_full = gains[6]

    patch_pos = patch_first + jnp.arange(patch_rows, dtype=jnp.int32)
    header_mask = (
        (patch_pos[None, :] < header_total[:, None]).astype(F32).reshape(patch_flat, 1)
    )
    patch_start = patch_rows_in.astype(F32).reshape(patch_flat, D) + header_mask * header_full
    patch_start, (text_input, patch_cotangent, text_cotangent) = in_order(
        patch_start, (text_input, patch_cotangent, text_cotangent)
    )
    text_rows_in = take_items(text_input)
    patch_grad_in = take_items(patch_cotangent)
    text_grad_in = take_items(text_cotangent)
    attn_input = rms_norm(patch_start, gains[0])
    enc_qkv = (
        matmul(attn_input, first_group[:, : 3 * D])
        .astype(BF16)
        .reshape(items, patch_rows, 3 * D)
    )
    enc_sides = split_of(enc_qkv)
    enc_attended, enc_exact, enc_total = attend_forward(*enc_sides, patch_scalars, False, swapped)
    attn_input, enc_attended = in_order(attn_input, enc_attended)
    attn_turned = turn_rows(attn_input)
    (text_rows_in, patch_grad_in, text_grad_in, attn_turned), enc_attended = in_order(
        (text_rows_in, patch_grad_in, text_grad_in, attn_turned), enc_attended
    )
    enc_attended_flat = enc_attended.reshape(patch_flat, D)
    (
        patch_middle,
        mlp_input,
        enc_slopes,
        enc_hidden,
        patch_rounded,
        patch_final,
        memory_input,
        memory_turned,
    ) = layer_forward(enc_attended_flat, patch_start, second_group, gains, 1, 4)
    memory_input, (cross_output, dec_gate_up, dec_down) = in_order(
        memory_input, (cross_output, dec_gate_up, dec_down)
    )
    fourth_group = gather_layer(dec_gate_up, dec_down, cross_output)
    patch_sent, unused = send_rows(patch_rounded.reshape(items, patch_rows, D))

    text_start = text_rows_in.reshape(text_flat, D)
    self_input = rms_norm(text_start.astype(F32), gains[2])
    self_qkv = (
        matmul(self_input, part_of(second_group, self_project_at))
        .astype(BF16)
        .reshape(items, text_rows, 3 * D)
    )
    self_sides = split_of(self_qkv)
    self_attended, self_exact, self_total = attend_forward(*self_sides, text_scalars, True, swapped)
    self_attended_flat = self_attended.reshape(text_flat, D)
    text_middle = text_start.astype(F32) + matmul(
        self_attended_flat, part_of(third_group, self_output_at)
    )
    cross_input = rms_norm(text_middle, gains[3])
    cross_queries = (
        matmul(cross_input, part_of(third_group, cross_query_at))
        .astype(BF16)
        .reshape(items, text_rows, D)
    )
    memory_kv = all_keys(
        matmul(memory_input, part_of(third_group, cross_memory_at))
        .astype(BF16)
        .reshape(items, patch_rows, 2 * D)
    )
    cross_sides = ((cross_queries, 0), (memory_kv, 0), (memory_kv, 1))
    cross_attended, cross_exact, cross_total = attend_forward(*cross_sides, cross_scalars, False, swapped)
    cross_attended_flat = cross_attended.reshape(text_flat, D)
    patch_sent, cross_attended_flat = in_order(patch_sent, cross_attended_flat)
    text_late, ffn_input, ffn_slopes, ffn_hidden, text_rounded = layer_forward(
        cross_attended_flat, text_middle, fourth_group, gains, 5
    )
    text_sent, unused = send_rows(text_rounded.reshape(items, text_rows, D))

    ffn_out_grad = text_grad_in.reshape(text_flat, D)
    ffn_gate_grad, late_grad, cross_out_grad, cross_head_grad, gain_ffn = layer_backward(
        ffn_out_grad, ffn_slopes, text_late, fourth_group, gains, 5
    )
    cross_head_grad = cross_head_grad.reshape(items, text_rows, D)
    first_width = 2 * FF + FF
    first_terms = fill_weight_grad(None, first_width, 0, ffn_input, ffn_gate_grad, True)
    first_terms = fill_down_grad(
        first_terms, first_width, 2 * FF, shard_rows, ffn_hidden, ffn_out_grad
    )
    first_terms, (cross_out_grad, cross_head_grad) = in_order(
        first_terms, (cross_out_grad, cross_head_grad)
    )
    first_sum = scatter(first_terms)

    second_width = 4 * D
    second_terms = fill_weight_grad(None, second_width, 0, cross_attended_flat, cross_out_grad)
    query_grad, key_grad = attend_backward(
        *cross_sides,
        cross_head_grad,
        cross_exact,
        cross_total,
        cross_scalars,
        False,
        swapped,
    )
    cross_query_grad = query_grad.reshape(text_flat, D)
    memory_kv_grad = own_keys(key_grad).reshape(patch_flat, 2 * D)
    second_terms = fill_weight_grad(second_terms, second_width, D, cross_input, cross_query_grad)
    second_terms = fill_weight_grad(
        second_terms, second_width, 2 * D, memory_turned, memory_kv_grad, True
    )
    second_terms, (cross_query_grad, memory_kv_grad) = in_order(
        second_terms, (cross_query_grad, memory_kv_grad)
    )
    second_sum = scatter(second_terms)
    middle_grad, gain_cross, self_out_grad, self_head_grad = project_back(
        [(cross_query_grad, third_group, cross_query_at)],
        late_grad,
        text_middle,
        gains,
        3,
        True,
        (third_group, self_output_at),
    )
    self_head_grad = self_head_grad.reshape(items, text_rows, D)

    self_terms = fill_weight_grad(None, second_width, 0, self_attended_flat, self_out_grad)
    self_qkv_grad = joined(
        attend_backward(
            *self_sides, self_head_grad, self_exact, self_total, text_scalars, True, swapped
        )
    )
    self_terms = fill_weight_grad(self_terms, second_width, D, self_input, self_qkv_grad)
    (self_terms, first_sum, text_sent), (self_qkv_grad, memory_kv_grad) = in_order(
        (self_terms, first_sum, text_sent), (self_qkv_grad, memory_kv_grad)
    )
    self_sum = scatter(self_terms)

    patch_grad, gain_memory, down_grad = project_back(
        [(memory_kv_grad, third_group, cross_memory_at)],
        patch_grad_in.reshape(patch_flat, D),
        patch_final,
        gains,
        4,
        True,
    )
    enc_gate_grad, enc_middle_grad, enc_out_grad, enc_head_grad, gain_mlp = layer_backward(
        patch_grad, enc_slopes, patch_middle, second_group, gains, 1
    )
    enc_head_grad = enc_head_grad.reshape(items, patch_rows, D)
    third_width = 2 * FF + FF
    third_terms = fill_weight_grad(None, third_width, 0, mlp_input, enc_gate_grad, True)
    third_terms = fill_down_grad(
        third_terms, third_width, 2 * FF, shard_rows, enc_hidden, down_grad
    )
    (third_terms, second_sum), (enc_out_grad, enc_head_grad) = in_order(
        (third_terms, second_sum), (enc_out_grad, enc_head_grad)
    )
    third_sum = scatter(third_terms)
    fourth_width = D + 3 * D
    fourth_terms = fill_weight_grad(None, fourth_width, 0, enc_attended_flat, enc_out_grad)
    grad_dec_gate_up, grad_dec_down = finish(first_sum, (2 * FF, FF))
    grad_cross_output, grad_cross_query, grad_memory_kv = finish(second_sum, (D, D, 2 * D))
    text_back, gain_self = project_back(
        [(self_qkv_grad, second_group, self_project_at)], middle_grad, text_start, gains, 2
    )
    text_back_sent, unused = send_rows(text_back.reshape(items, text_rows, D))
    fourth_terms, enc_head_grad = in_order(fourth_terms, enc_head_grad)

    enc_qkv_grad = joined(
        attend_backward(
            *enc_sides, enc_head_grad, enc_exact, enc_total, patch_scalars, False, swapped
        )
    )
    late = (
        text_back_sent,
        gain_self,
        self_sum,
        third_sum,
        grad_dec_gate_up,
        grad_dec_down,
        grad_cross_output,
        grad_cross_query,
        grad_memory_kv,
    )
    late, enc_qkv_grad = in_order(late, enc_qkv_grad)
    (
        text_back_sent,
        gain_self,
        self_sum,
        third_sum,
        grad_dec_gate_up,
        grad_dec_down,
        grad_cross_output,
        grad_cross_query,
        grad_memory_kv,
    ) = late
    fourth_terms = fill_weight_grad(
        fourth_terms, fourth_width, D, attn_turned, enc_qkv_grad, True
    )
    fourth_terms, enc_qkv_grad = in_order(fourth_terms, enc_qkv_grad)
    fourth_sum = scatter(fourth_terms)
    self_got, third_got = exchange(self_sum), exchange(third_sum)
    (self_got, third_got), enc_qkv_grad = in_order((self_got, third_got), enc_qkv_grad)

    start_grad, gain_attn = project_back(
        [(enc_qkv_grad, first_group, (3 * D, 0))], enc_middle_grad, patch_start, gains, 0
    )
    patch_back_sent, start_grad = send_rows(
        start_grad.reshape(items, patch_rows, D), start_grad
    )
    header_term = jnp.sum(start_grad * header_mask, axis=0, keepdims=True)
    terms = (gain_attn, gain_mlp, gain_self, gain_cross, gain_memory, gain_ffn, header_term)
    small_term = jnp.concatenate([term[:1] for term in terms + (jnp.zeros_like(header_term),)])
    small_own = lax.dynamic_slice_in_dim(
        sum_small(small_term), lax.axis_index("wide") * shard_rows, shard_rows, 1
    ).T
    small_own = jnp.pad(small_own.astype(BF16), ((0, 0), (0, PAIR - small_own.shape[1])))

    grad_self_output, grad_self_project = finish(self_sum, (D, 3 * D), self_got)
    grad_enc_gate_up, grad_enc_down = finish(third_sum, (2 * FF, FF), third_got)
    grad_enc_output, grad_enc_project, grad_small = finish(
        jnp.concatenate([fourth_sum, small_own], axis=1), (D, 3 * D, PAIR)
    )
    patch_output = place_rows(patch_sent)
    text_output = place_rows(text_sent)
    text_input_grad = place_rows(text_back_sent)
    patch_input_grad = place_rows(patch_back_sent)
    grad_cross_project = jnp.concatenate([grad_cross_query, by_side(grad_memory_kv)], axis=1)
    return (
        patch_output,
        text_output,
        patch_input_grad,
        text_input_grad,
        grad_small[:, :6],
        grad_small[:, 6],
        by_side(grad_enc_project),
        grad_enc_output,
        by_half(grad_enc_gate_up),
        rows_to_down(grad_enc_down),
        by_side(grad_self_project),
        grad_self_output,
        grad_cross_project,
        grad_cross_output,
        by_half(grad_dec_gate_up),
        rows_to_down(grad_dec_down),
    )


def solution(mesh):
    rows = P("wide", "narrow", None)
    weight = P("wide", None)
    vector = P("wide")
    return jax.shard_map(
        functools.partial(on_device, mesh.shape["narrow"]),
        mesh=mesh,
        in_specs=(rows,) * 4 + (vector,) * 3 + (weight, vector) + (weight,) * 10,
        out_specs=(rows,) * 4 + (weight, vector) + (weight,) * 10,
        check_vma=False,
    )
```

```python
import functools
import math

import jax
import jax.numpy as jnp
from jax import lax
from jax.experimental import pallas as pl
from jax.experimental.pallas import tpu as pltpu
from jax.sharding import PartitionSpec as P

D = 768
HEADS = 12
HEAD_DIM = 64
FF = 2048
PAIR = 2 * HEAD_DIM
PAIRS = HEADS // 2
FF_BLOCK = 256
GELU_SCALE = 0.7978845608028654
GELU_CUBE = 0.044715


EPSILON = 1e-06
NEGATIVE = -1e30
BF16 = jnp.bfloat16
F32 = jnp.float32


def rms_scale(values):
    return lax.rsqrt(jnp.mean(values * values, axis=-1, keepdims=True) + EPSILON)


def rms_norm(values, gain_row):
    inverse = rms_scale(values)
    return (values * inverse * gain_row).astype(BF16)


def matmul(left_side, right_side):
    return jnp.dot(left_side, right_side, preferred_element_type=F32)


def matmul_back(left_side, right_side):
    return lax.dot_general(
        left_side, right_side, (((1,), (1,)), ((), ())), preferred_element_type=F32
    )


def dot(left_side, right_side):
    return jnp.dot(left_side, right_side, preferred_element_type=F32)


def lanes_of(rows):
    return lax.broadcasted_iota(jnp.int32, (rows, PAIR), 1)


def place(lane, first_lane, columns):
    filled = jnp.zeros(lane.shape, F32)
    for offset, column in enumerate(columns):
        filled = jnp.where(lane == first_lane + offset, column, filled)
    return filled


def three_parts(values):
    high = values.astype(BF16).astype(F32)
    rest = values - high
    middle = rest.astype(BF16).astype(F32)
    return (high, middle, (rest - middle).astype(BF16).astype(F32))


def both_heads(lane, pair_values, columns):
    first = jnp.where(lane < HEAD_DIM, pair_values, place(lane, HEAD_DIM, columns))
    second = jnp.where(lane >= HEAD_DIM, pair_values, place(lane, 0, columns))
    return (first.astype(BF16), second.astype(BF16))


def key_bias(first_key, rows, limit):
    position = first_key + lax.broadcasted_iota(jnp.int32, (rows, PAIR), 0)
    return jnp.where(position < limit, 0.0, NEGATIVE)


def forward_kernel(
    causal,
    aligned,
    scalars_ref,
    query_ref,
    key_ref,
    value_ref,
    out_ref,
    exact_ref,
    total_ref,
    key_first,
    key_second,
    value_first,
    value_second,
    key_bound,
):
    item = pl.program_id(0)
    block = pl.program_id(2)
    block_rows = query_ref.shape[1]
    key_total = key_ref.shape[1]
    limit = scalars_ref[1 + item]
    query_start = scalars_ref[0]

    def longest(lane, pair_values):
        square = pair_values * pair_values
        first = jnp.sum(jnp.where(lane < HEAD_DIM, square, 0.0), axis=1, keepdims=True)
        second = jnp.sum(jnp.where(lane >= HEAD_DIM, square, 0.0), axis=1, keepdims=True)
        return (jnp.max(first), jnp.max(second))

    @pl.when(block == 0)
    def prepare():
        lane = lanes_of(key_total)
        pair_keys = key_ref[0].astype(F32)
        keys = both_heads(lane, pair_keys, (key_bias(0, key_total, limit),))
        key_first[...] = keys[0].T
        key_second[...] = keys[1].T
        values = value_ref[0].astype(F32)
        value_first[...] = jnp.where(lane < HEAD_DIM, values, 1.0).astype(BF16)
        value_second[...] = jnp.where(lane >= HEAD_DIM, values, 1.0).astype(BF16)
        bounds = longest(lane, pair_keys)
        key_bound[0] = bounds[0]
        key_bound[1] = bounds[1]

    lane = lanes_of(block_rows)
    own = lane < HEAD_DIM
    scaled = query_ref[0].astype(F32) * HEAD_DIM ** (-0.5)
    queries = both_heads(lane, scaled, (1.0,))
    bounds = longest(lane, scaled)
    bound = jnp.maximum(bounds[0] * key_bound[0], bounds[1] * key_bound[1])
    sides = ((queries[0], key_first, value_first), (queries[1], key_second, value_second))

    def score_piece(head_queries, head_keys, piece):
        first_key, width, masked = piece
        scores = dot(head_queries, head_keys[:, first_key : first_key + width])
        if masked:
            row_pos = (
                query_start
                + block * block_rows
                + lax.broadcasted_iota(jnp.int32, (block_rows, width), 0)
            )
            key_pos = first_key + lax.broadcasted_iota(jnp.int32, (block_rows, width), 1)
            scores = jnp.where(key_pos <= row_pos, scores, NEGATIVE)
        return scores

    def store(sums, shifts):
        row_sum = pltpu.roll(jnp.where(own, sums[1], sums[0]), HEAD_DIM, 1)
        exact = jnp.where(own, sums[0], sums[1]) / row_sum
        exact_ref[0] = exact
        out_ref[0] = exact.astype(BF16)
        total_ref[0] = jnp.where(own, shifts[0], shifts[1]) + jnp.log(row_sum)

    def unshifted(pieces):
        units = [(piece, side) for piece in pieces for side in range(2)]

        def scores_of(unit):
            piece, side = unit
            return score_piece(sides[side][0], sides[side][1], piece)

        sums = [None, None]
        ahead = scores_of(units[0])
        for index, (piece, side) in enumerate(units):
            scores = ahead
            if index + 1 < len(units):
                ahead = scores_of(units[index + 1])
            weights = jnp.exp(scores).astype(BF16)
            term = dot(weights, sides[side][2][piece[0] : piece[0] + piece[1], :])
            sums[side] = term if sums[side] is None else sums[side] + term
        store(sums, (0.0, 0.0))

    def shifted(pieces):
        sums = []
        shifts = []
        for head_queries, head_keys, head_values in sides:
            scores = [score_piece(head_queries, head_keys, piece) for piece in pieces]
            row_max = None
            for part in scores:
                part_max = jnp.max(part, axis=1, keepdims=True)
                row_max = part_max if row_max is None else jnp.maximum(row_max, part_max)
            summed = None
            for piece, part in zip(pieces, scores):
                weights = jnp.exp(part - row_max).astype(BF16)
                term = dot(weights, head_values[piece[0] : piece[0] + piece[1], :])
                summed = term if summed is None else summed + term
            sums.append(summed)
            shifts.append(row_max)
        store(sums, shifts)

    def run(pieces):
        @pl.when(bound <= 1600.0)
        def plain():
            unshifted(pieces)

        @pl.when(bound > 1600.0)
        def general():
            shifted(pieces)

    def whole_row(masked):
        step = min(512, key_total)
        return [(first, step, masked) for first in range(0, key_total, step)]

    if not causal:
        run(whole_row(False))
    elif not aligned:
        run(whole_row(True))
    else:
        for index in range(key_total // block_rows):

            @pl.when(block == index)
            def one_block(index=index):
                first_key = index * block_rows
                pieces = [(0, first_key, False)] if index else []
                run(pieces + [(first_key, block_rows, True)])


def backward_kernel(
    causal,
    aligned,
    chunk_rows,
    scalars_ref,
    query_ref,
    key_ref,
    value_ref,
    grad_ref,
    exact_ref,
    total_ref,
    *refs,
):
    if len(refs) == 9:
        query_grad_ref, key_grad_ref = refs[:2]
        key_at = 0
    else:
        query_grad_ref = key_grad_ref = refs[0]
        key_at = PAIR
    (
        query_first,
        query_second,
        grad_first,
        grad_second,
        query_across,
        grad_across,
        query_sum,
    ) = refs[-7:]
    item = pl.program_id(0)
    block = pl.program_id(2)
    query_total = query_ref.shape[1]
    block_keys = key_ref.shape[1]
    limit = scalars_ref[1 + item]
    query_start = scalars_ref[0]
    scale = HEAD_DIM ** (-0.5)

    @pl.when(block == 0)
    def prepare():
        lane = lanes_of(query_total)
        own = lane < HEAD_DIM
        scaled = query_ref[0].astype(F32) * scale
        query_across[...] = scaled.astype(BF16).T
        total = -pltpu.roll(total_ref[0], HEAD_DIM, 1)
        queries = both_heads(lane, scaled, (1.0,) + three_parts(total))
        query_first[...] = queries[0]
        query_second[...] = queries[1]
        grads = grad_ref[0].astype(F32)
        grad_across[...] = grad_ref[0].T
        product = grads * exact_ref[0]
        first_sum = jnp.sum(jnp.where(own, product, 0.0), axis=1, keepdims=True)
        second_sum = jnp.sum(jnp.where(own, 0.0, product), axis=1, keepdims=True)
        weighted = -jnp.where(own, second_sum, first_sum)
        head_grads = both_heads(lane, grads, three_parts(weighted))
        grad_first[...] = head_grads[0]
        grad_second[...] = head_grads[1]
        query_sum[...] = jnp.zeros_like(query_sum)

    lane = lanes_of(block_keys)
    bias = key_bias(block * block_keys, block_keys, limit)
    pair_keys = key_ref[0].astype(F32)
    keys = [part.T for part in both_heads(lane, pair_keys, (bias, 1.0, 1.0, 1.0))]
    values = [
        part.T for part in both_heads(lane, value_ref[0].astype(F32), (1.0, 1.0, 1.0))
    ]
    keys_across = (pair_keys * scale).astype(BF16).T

    def run(pieces):
        key_parts = [None, None]
        value_parts = [None, None]
        units = [(piece, head) for piece in pieces for head in range(2)]
        sides = ((query_first, grad_first), (query_second, grad_second))

        def products_of(unit):
            (first_row, width, masked), head = unit
            rows = slice(first_row, first_row + width)
            scores = dot(sides[head][0][rows, :], keys[head])
            if masked:
                row_pos = (
                    query_start
                    + first_row
                    + lax.broadcasted_iota(jnp.int32, (width, block_keys), 0)
                )
                key_pos = block * block_keys + lax.broadcasted_iota(
                    jnp.int32, (width, block_keys), 1
                )
                scores = jnp.where(key_pos <= row_pos, scores, NEGATIVE)
            return (scores, dot(sides[head][1][rows, :], values[head]))

        ahead = products_of(units[0])
        for index, ((first_row, width, masked), head) in enumerate(units):
            scores, weight_grad = ahead
            if index + 1 < len(units):
                ahead = products_of(units[index + 1])
            rows = slice(first_row, first_row + width)
            head_rows = slice(head * HEAD_DIM, (head + 1) * HEAD_DIM)
            weights = jnp.exp(scores)
            score_grad = (weights * weight_grad).astype(BF16)
            value_term = dot(grad_across[head_rows, rows], weights.astype(BF16))
            key_term = dot(query_across[head_rows, rows], score_grad)
            query_sum[head_rows, rows] += matmul_back(keys_across[head_rows, :], score_grad)
            if key_parts[head] is None:
                key_parts[head], value_parts[head] = key_term, value_term
            else:
                key_parts[head] = key_parts[head] + key_term
                value_parts[head] = value_parts[head] + value_term
        block_rows = pl.ds(pl.multiple_of(block * block_keys, block_keys), block_keys)
        key_grad_ref[0, block_rows, key_at : key_at + PAIR] = (
            jnp.concatenate(key_parts, axis=0).T.astype(BF16)
        )
        key_grad_ref[0, block_rows, key_at + PAIR : key_at + 2 * PAIR] = (
            jnp.concatenate(value_parts, axis=0).T.astype(BF16)
        )

    def chunks(first_row, masked):
        return [
            (start, min(chunk_rows, query_total - start), masked)
            for start in range(first_row, query_total, chunk_rows)
        ]

    if not causal:
        run(chunks(0, False))
    elif not aligned:
        run(chunks(0, True))
    else:
        for index in range(query_total // block_keys):

            @pl.when(block == index)
            def one_block(index=index):
                first_row = index * block_keys
                run(
                    [(first_row, block_keys, True)]
                    + chunks(first_row + block_keys, False)
                )

    @pl.when(block == pl.num_programs(2) - 1)
    def finish():
        query_grad_ref[0, :, :PAIR] = query_sum[...].T.astype(BF16)


VMEM_BYTES = 56 * 1024 * 1024
SMALL_COST = pl.CostEstimate(flops=1000, bytes_accessed=1000, transcendentals=0)


def row_scale(values):
    return lax.rsqrt(jnp.mean(values * values, axis=1, keepdims=True) + EPSILON)


def norm_back(gradient, values, gain):
    inverse = row_scale(values)
    unit = values * inverse
    gain_grad = jnp.sum(gradient * unit, axis=0, keepdims=True)
    scaled = gradient * gain
    inner_mean = jnp.mean(scaled * unit, axis=1, keepdims=True)
    return (inverse * (scaled - unit * inner_mean), gain_grad)


def add_rows(total_ref, row):
    @pl.when(pl.program_id(0) == 0)
    def start():
        total_ref[...] = jnp.zeros_like(total_ref)

    total_ref[0:1, :] += row


def unpack_down(packed_ref, down_ref):
    for device in range(16):
        for group in range(8):
            for column in range(D // 256):
                row = (device * 8 + group) * 16
                down_ref[row : row + 16, column * 256 : (column + 1) * 256] = packed_ref[
                    device * 48 + column * 16 : device * 48 + (column + 1) * 16,
                    group * 256 : (group + 1) * 256,
                ]


def layer_forward_kernel(
    gain_row,
    next_row,
    attended_ref,
    start_ref,
    gate_up_ref,
    packed_ref,
    output_ref,
    gains_ref,
    middle_ref,
    normed_ref,
    slopes_ref,
    hidden_ref,
    rounded_ref,
    *refs,
):
    rows_ref, down_ref = refs[-2:]

    @pl.when(pl.program_id(0) == 0)
    def unpack():
        unpack_down(packed_ref, down_ref)

    middle = start_ref[...].astype(F32) + dot(attended_ref[...], output_ref[...])
    middle_ref[...] = middle
    normed = (middle * row_scale(middle) * gains_ref[gain_row : gain_row + 1, :]).astype(BF16)
    normed_ref[...] = normed.T

    span = 2 * FF_BLOCK

    def product_of(first):
        return dot(normed, gate_up_ref[:, 2 * first : 2 * (first + span)])

    ahead = product_of(0)
    for start in range(0, FF, span):
        product = ahead
        if start + span < FF:
            ahead = product_of(start + span)
        for first in range(start, start + span, FF_BLOCK):
            both = product[:, 2 * (first - start) : 2 * (first - start + FF_BLOCK)]
            gate, up = both[:, :FF_BLOCK], both[:, FF_BLOCK:]
            square = gate * gate
            bend = jnp.tanh(gate * (GELU_SCALE + (GELU_SCALE * GELU_CUBE) * square))
            half = 0.5 + 0.5 * bend
            bent = gate * half
            slope = half + (1.0 - bend * bend) * (
                gate * (0.5 * GELU_SCALE + (1.5 * GELU_SCALE * GELU_CUBE) * square)
            )
            slopes_ref[:, 2 * first : 2 * first + FF_BLOCK] = (up * slope).astype(BF16)
            slopes_ref[:, 2 * first + FF_BLOCK : 2 * (first + FF_BLOCK)] = bent.astype(BF16)
            hidden = (bent * up).astype(BF16)
            rows_ref[:, first : first + FF_BLOCK] = hidden
            hidden_ref[first : first + FF_BLOCK, :] = hidden.T
    final = middle + dot(rows_ref[...], down_ref[...])
    rounded_ref[...] = final.astype(BF16)
    if next_row is not None:
        refs[0][...] = final
        next_normed = (
            final * row_scale(final) * gains_ref[next_row : next_row + 1, :]
        ).astype(BF16)
        refs[1][...] = next_normed
        refs[2][...] = next_normed.T


def layer_backward_kernel(
    gain_row,
    grad_ref,
    slopes_ref,
    middle_ref,
    gate_up_ref,
    packed_ref,
    output_ref,
    gains_ref,
    gate_grad_ref,
    middle_grad_ref,
    rounded_ref,
    head_grad_ref,
    gain_grad_ref,
    down_ref,
):
    @pl.when(pl.program_id(0) == 0)
    def unpack():
        unpack_down(packed_ref, down_ref)

    out_grad = grad_ref[...].astype(BF16)

    span = 2 * FF_BLOCK

    def product_of(first):
        return matmul_back(out_grad, down_ref[first : first + span, :])

    ahead = product_of(0)
    for start in range(0, FF, span):
        product = ahead
        if start + span < FF:
            ahead = product_of(start + span)
        for first in range(start, start + span, FF_BLOCK):
            both = slice(2 * first, 2 * (first + FF_BLOCK))
            hidden_grad = product[:, first - start : first - start + FF_BLOCK]
            hidden_grad = jnp.concatenate([hidden_grad, hidden_grad], axis=1)
            gate_grad_ref[:, both] = (hidden_grad * slopes_ref[:, both].astype(F32)).astype(BF16)
    normed_grad = matmul_back(gate_grad_ref[...], gate_up_ref[...])
    in_grad, gain_grad = norm_back(
        normed_grad, middle_ref[...], gains_ref[gain_row : gain_row + 1, :]
    )
    add_rows(gain_grad_ref, gain_grad)
    middle_grad = grad_ref[...].astype(F32) + in_grad
    middle_grad_ref[...] = middle_grad
    rounded = middle_grad.astype(BF16)
    rounded_ref[...] = rounded
    head_grad_ref[...] = matmul_back(rounded, output_ref[...]).astype(BF16)


def project_back_kernel(gain_row, sides, with_rounded, with_head, *refs):
    grads, weights = refs[:sides], refs[sides : 2 * sides]
    base_ref, values_ref, gains_ref = refs[2 * sides : 2 * sides + 3]
    outs = list(refs[2 * sides + 3 :])
    output_ref = outs.pop(0) if with_head else None
    normed_grad = None
    for grad_ref, weight_ref in zip(grads, weights):
        term = matmul_back(grad_ref[...], weight_ref[...])
        normed_grad = term if normed_grad is None else normed_grad + term
    in_grad, gain_grad = norm_back(
        normed_grad, values_ref[...].astype(F32), gains_ref[gain_row : gain_row + 1, :]
    )
    total = base_ref[...].astype(F32) + in_grad
    outs[0][...] = total
    add_rows(outs[1], gain_grad)
    if with_rounded:
        rounded = total.astype(BF16)
        outs[2][...] = rounded
        if with_head:
            outs[3][...] = matmul_back(rounded, output_ref[...]).astype(BF16)


def rows_call(kernel, rows, operands, outs, scratch, name):
    step = min(512, rows)
    in_specs = []
    for array, stays in operands:
        if stays is None:
            in_specs.append(pl.BlockSpec((step, array.shape[1]), lambda m: (m, 0)))
        else:
            width, column = stays
            in_specs.append(
                pl.BlockSpec(
                    (array.shape[0], width),
                    functools.partial(lambda at, m: (0, at), column // width),
                    pipeline_mode=pl.Buffered(1),
                )
            )
    out_specs = []
    out_shape = []
    for width, dtype, *across in outs:
        if across:
            out_specs.append(pl.BlockSpec((width, step), lambda m: (0, m)))
            out_shape.append(jax.ShapeDtypeStruct((width, rows), dtype))
        elif dtype is None:
            out_specs.append(pl.BlockSpec((8, width), lambda m: (0, 0)))
            out_shape.append(jax.ShapeDtypeStruct((8, width), F32))
        else:
            out_specs.append(pl.BlockSpec((step, width), lambda m: (m, 0)))
            out_shape.append(jax.ShapeDtypeStruct((rows, width), dtype))
    return pl.pallas_call(
        kernel,
        grid=(rows // step,),
        in_specs=in_specs,
        out_specs=out_specs,
        out_shape=out_shape,
        scratch_shapes=scratch,
        compiler_params=pltpu.CompilerParams(vmem_limit_bytes=VMEM_BYTES),
        cost_estimate=SMALL_COST,
        name=name,
    )(*[array for array, stays in operands])


LAYER_SIDES = ((2 * FF, 0), (FF, 2 * FF), (D, 3 * FF))


def layer_forward(attended, start, layer, gains, gain_row, next_row=None):
    outs = [(D, F32), (D, BF16, True), (2 * FF, BF16), (FF, BF16, True), (D, BF16)]
    if next_row is not None:
        outs += [(D, F32), (D, BF16), (D, BF16, True)]
    return rows_call(
        functools.partial(layer_forward_kernel, gain_row, next_row),
        attended.shape[0],
        [(attended, None), (start, None)]
        + [(layer, side) for side in LAYER_SIDES]
        + [(gains, (D, 0))],
        outs,
        [pltpu.VMEM((min(512, attended.shape[0]), FF), BF16), pltpu.VMEM((FF, D), BF16)],
        "layer_forward",
    )


def layer_backward(grad, slopes, middle, layer, gains, gain_row):
    return rows_call(
        functools.partial(layer_backward_kernel, gain_row),
        grad.shape[0],
        [(grad, None), (slopes, None), (middle, None)]
        + [(layer, side) for side in LAYER_SIDES]
        + [(gains, (D, 0))],
        [(2 * FF, BF16), (D, F32), (D, BF16), (D, BF16), (D, None)],
        [pltpu.VMEM((FF, D), BF16)],
        "layer_backward",
    )


def project_back(sides, base, values, gains, gain_row, rounded=False, output=None):
    operands = [(grad, None) for grad, weight, place in sides]
    operands += [(weight, place) for grad, weight, place in sides]
    operands += [(base, None), (values, None), (gains, (D, 0))]
    outs = [(D, F32), (D, None)]
    if rounded:
        outs.append((D, BF16))
    if output is not None:
        operands.append(output)
        outs.append((D, BF16))
    return rows_call(
        functools.partial(
            project_back_kernel, gain_row, len(sides), rounded, output is not None
        ),
        base.shape[0],
        operands,
        outs,
        [],
        "project_back",
    )


def weight_grad_kernel(left_ref, right_ref, *refs):
    out_ref, across = refs[-2:]

    @pl.when(pl.program_id(0) == 0)
    def turn():
        step = min(256, left_ref.shape[0])
        for first_row in range(0, left_ref.shape[0], step):
            across[:, first_row : first_row + step] = left_ref[first_row : first_row + step, :].T

    out_ref[...] = dot(across[...], right_ref[...]).astype(BF16)


def turned_grad_kernel(left_ref, right_ref, *refs):
    refs[-1][...] = dot(left_ref[...], right_ref[...]).astype(BF16)


def turn_kernel(rows_ref, out_ref):
    out_ref[...] = rows_ref[...].T


def turn_rows(array):
    return rows_call(
        turn_kernel, array.shape[0], [(array, None)], [(array.shape[1], BF16, True)], [], "turn_rows"
    )[0]


def down_grad_kernel(shard_rows, hidden_ref, right_ref, *refs):
    out_ref = refs[-1]
    term = dot(hidden_ref[...], right_ref[...]).astype(BF16)
    group_rows = FF * shard_rows // D // 8
    for device in range(out_ref.shape[0] // shard_rows):
        for column in range(D // 256):
            for group in range(8):
                first_row = (device * 8 + group) * group_rows
                out_row = device * shard_rows + column * group_rows
                out_ref[out_row : out_row + group_rows, group * 256 : (group + 1) * 256] = term[
                    first_row : first_row + group_rows, column * 256 : (column + 1) * 256
                ]


def fill_call(kernel, grid, in_specs, out_spec, columns, scratch, operands, buffer, name):
    operands = list(operands)
    in_specs = list(in_specs)
    aliases = {}
    if buffer is not None:
        aliases = {len(operands): 0}
        operands.append(buffer)
        in_specs.append(pl.BlockSpec(memory_space=pl.ANY))
    return pl.pallas_call(
        kernel,
        grid=grid,
        in_specs=in_specs,
        out_specs=out_spec,
        out_shape=jax.ShapeDtypeStruct((D, columns), BF16),
        scratch_shapes=scratch,
        input_output_aliases=aliases,
        compiler_params=pltpu.CompilerParams(vmem_limit_bytes=VMEM_BYTES),
        cost_estimate=SMALL_COST,
        name=name,
    )(*operands)


def fill_weight_grad(buffer, columns, first_column, left_side, right_side, turned=False):
    rows = right_side.shape[0]
    step = 1024 if right_side.shape[1] % 1024 == 0 else D
    first_step = first_column // step
    return fill_call(
        turned_grad_kernel if turned else weight_grad_kernel,
        (right_side.shape[1] // step,),
        [
            pl.BlockSpec(left_side.shape, lambda n: (0, 0)),
            pl.BlockSpec((rows, step), lambda n: (0, n)),
        ],
        pl.BlockSpec((D, step), lambda n: (0, first_step + n)),
        columns,
        [] if turned else [pltpu.VMEM((D, rows), BF16)],
        (left_side, right_side),
        buffer,
        "weight_grad",
    )


def fill_down_grad(buffer, columns, first_column, shard_rows, hidden, out_grad):
    rows = out_grad.shape[0]
    wide = D // shard_rows
    if FF // wide // 8 % 16:
        cut = matmul(hidden, out_grad).astype(BF16).reshape(wide, 8, FF // wide // 8, 3, 256)
        cut = cut.transpose(0, 3, 2, 1, 4).reshape(D, FF)
        return lax.dynamic_update_slice(buffer, cut, (0, first_column))
    devices = math.gcd(wide, 4)
    first_step = first_column // FF
    return fill_call(
        functools.partial(down_grad_kernel, shard_rows),
        (wide // devices,),
        [
            pl.BlockSpec((devices * FF // wide, rows), lambda n: (n, 0)),
            pl.BlockSpec((rows, D), lambda n: (0, 0)),
        ],
        pl.BlockSpec((devices * shard_rows, FF), lambda n: (n, first_step)),
        columns,
        [],
        (hidden, out_grad),
        buffer,
        "down_grad",
    )


def attend_forward(query_side, key_side, value_side, scalars, causal, aligned):
    (query_array, query_at), (key_array, key_at), (value_array, value_at) = (
        query_side,
        key_side,
        value_side,
    )
    query_step, key_step = query_array.shape[2] // D, key_array.shape[2] // D
    items, rows = query_array.shape[0], query_array.shape[1]
    keys = key_array.shape[1]
    block_rows = min(512 if causal else 1024, rows)
    return pl.pallas_call(
        functools.partial(forward_kernel, causal, aligned),
        grid=(items, PAIRS, rows // block_rows),
        in_specs=[
            pl.BlockSpec(memory_space=pltpu.SMEM),
            pl.BlockSpec((1, block_rows, PAIR), lambda i, p, b: (i, b, query_at + query_step * p)),
            pl.BlockSpec((1, keys, PAIR), lambda i, p, b: (i, 0, key_at + key_step * p)),
            pl.BlockSpec((1, keys, PAIR), lambda i, p, b: (i, 0, value_at + key_step * p)),
        ],
        out_specs=[
            pl.BlockSpec((1, block_rows, PAIR), lambda i, p, b: (i, b, p)),
            pl.BlockSpec((1, block_rows, PAIR), lambda i, p, b: (i, b, p)),
            pl.BlockSpec((1, block_rows, PAIR), lambda i, p, b: (i, b, p)),
        ],
        out_shape=[
            jax.ShapeDtypeStruct((items, rows, D), BF16),
            jax.ShapeDtypeStruct((items, rows, D), F32),
            jax.ShapeDtypeStruct((items, rows, D), F32),
        ],
        scratch_shapes=[
            pltpu.VMEM((PAIR, keys), BF16),
            pltpu.VMEM((PAIR, keys), BF16),
            pltpu.VMEM((keys, PAIR), BF16),
            pltpu.VMEM((keys, PAIR), BF16),
            pltpu.SMEM((2,), F32),
        ],
        compiler_params=pltpu.CompilerParams(vmem_limit_bytes=VMEM_BYTES),
        cost_estimate=SMALL_COST,
        name="attend_forward",
    )(scalars, query_array, key_array, value_array)


def attend_backward(
    query_side,
    key_side,
    value_side,
    head_grad,
    exact,
    total,
    scalars,
    causal,
    aligned,
    first_pair=0,
    pairs=PAIRS,
    block_keys=512,
    chunk_rows=1024,
):
    (query_array, query_at), (key_array, key_at), (value_array, value_at) = (
        query_side,
        key_side,
        value_side,
    )
    query_step, key_step = query_array.shape[2] // D, key_array.shape[2] // D
    items, rows = query_array.shape[0], query_array.shape[1]
    keys = key_array.shape[1]
    chunk_rows = min(chunk_rows, rows)
    whole = pl.BlockSpec((1, rows, PAIR), lambda i, p, b: (i, 0, first_pair + p))
    together = query_array is key_array
    if together:
        widths = ((rows, 3 * PAIR),)
    else:
        widths = ((rows, PAIR), (keys, 2 * PAIR))
    return pl.pallas_call(
        functools.partial(backward_kernel, causal, aligned, chunk_rows),
        grid=(items, pairs, keys // block_keys),
        in_specs=[
            pl.BlockSpec(memory_space=pltpu.SMEM),
            pl.BlockSpec((1, rows, PAIR), lambda i, p, b: (i, 0, query_at + query_step * (first_pair + p))),
            pl.BlockSpec((1, block_keys, PAIR), lambda i, p, b: (i, b, key_at + key_step * (first_pair + p))),
            pl.BlockSpec((1, block_keys, PAIR), lambda i, p, b: (i, b, value_at + key_step * (first_pair + p))),
            whole,
            whole,
            whole,
        ],
        out_specs=[pl.BlockSpec((1,) + width, lambda i, p, b: (i, 0, p)) for width in widths],
        out_shape=[
            jax.ShapeDtypeStruct((items, width[0], width[1] * pairs), BF16) for width in widths
        ],
        scratch_shapes=[
            pltpu.VMEM((rows, PAIR), BF16),
            pltpu.VMEM((rows, PAIR), BF16),
            pltpu.VMEM((rows, PAIR), BF16),
            pltpu.VMEM((rows, PAIR), BF16),
            pltpu.VMEM((PAIR, rows), BF16),
            pltpu.VMEM((PAIR, rows), BF16),
            pltpu.VMEM((PAIR, rows), F32),
        ],
        compiler_params=pltpu.CompilerParams(vmem_limit_bytes=VMEM_BYTES),
        cost_estimate=SMALL_COST,
        name="attend_backward",
    )(scalars, query_array, key_array, value_array, head_grad, exact, total)


def place_kernel(spot_ref, own_ref, got_ref, out_ref):
    slot = pl.program_id(1)

    @pl.when(slot == spot_ref[0])
    def keep():
        out_ref[0] = own_ref[...]

    @pl.when(slot != spot_ref[0])
    def take():
        out_ref[0] = got_ref[...].astype(out_ref.dtype)


def place_halves(spot, array, got):
    half = got.shape[0]
    step = min(512, half)
    blocks = half // step
    return pl.pallas_call(
        place_kernel,
        grid_spec=pltpu.PrefetchScalarGridSpec(
            num_scalar_prefetch=1,
            grid=(blocks, 2),
            in_specs=[
                pl.BlockSpec((step, D), lambda m, i, spot_ref: (spot_ref[0] * blocks + m, 0)),
                pl.BlockSpec((step, D), lambda m, i, spot_ref: (m, 0)),
            ],
            out_specs=pl.BlockSpec((1, step, D), lambda m, i, spot_ref: (i, m, 0)),
        ),
        out_shape=jax.ShapeDtypeStruct((2, half, D), array.dtype),
        compiler_params=pltpu.CompilerParams(vmem_limit_bytes=VMEM_BYTES),
        cost_estimate=pl.CostEstimate(flops=1000, bytes_accessed=24000000, transcendentals=0),
        name="place_halves",
    )(spot.astype(jnp.int32).reshape(1), array, got)


def in_order(first, second):
    return lax.optimization_barrier((first, second))


def on_device(
    narrow,
    patch_input,
    text_input,
    patch_cotangent,
    text_cotangent,
    patch_count,
    header_len,
    text_len,
    norm_gains,
    header_embed,
    enc_project,
    enc_output,
    enc_gate_up,
    enc_down,
    self_project,
    self_output,
    cross_project,
    cross_output,
    dec_gate_up,
    dec_down,
):
    swapped = narrow == 2 and patch_input.shape[0] == 2
    spot = lax.axis_index("narrow")
    shard_rows = norm_gains.shape[0]
    wide = D // shard_rows

    def partner(array):
        return lax.ppermute(array, "narrow", [(0, 1), (1, 0)])

    def pick(own, got, position):
        slot = jnp.arange(2, dtype=jnp.int32).reshape(2, 1, 1)
        return jnp.where(slot == position, own[None], got[None])

    def take_items(array):
        if not swapped:
            return array
        own = lax.dynamic_index_in_dim(array, spot, 0, keepdims=False)
        got = partner(lax.dynamic_index_in_dim(array, 1 - spot, 0, keepdims=False))
        return pick(own, got, spot).reshape(1, -1, D)

    def halve_rows(array):
        half = array.shape[1] // 2
        own = lax.dynamic_slice_in_dim(array[0], spot * half, half, 0)
        away = lax.dynamic_slice_in_dim(array[0], (1 - spot) * half, half, 0)
        return (own, away.astype(BF16))

    def send_rows(array, tied=None):
        if not swapped:
            return (array, None), tied
        own, away = halve_rows(array)
        away, tied = in_order(away, tied)
        return (own, partner(away)), tied

    def place_rows(sent):
        own, got = sent
        return own if got is None else pick(own, got.astype(own.dtype), spot)

    def gather(*arrays):
        whole = jnp.concatenate(arrays, axis=1) if len(arrays) > 1 else arrays[0]
        return lax.all_gather(whole, "wide", axis=0, tiled=True)

    def scatter(summed):
        return lax.psum_scatter(summed, "wide", scatter_dimension=0, tiled=True)

    def sum_small(array):
        step = 1
        while step < wide:
            ways = min(4, wide // step)
            got = [
                lax.ppermute(
                    array, "wide", [(index, index ^ (step * way)) for index in range(wide)]
                )
                for way in range(1, ways)
            ]
            array = functools.reduce(jnp.add, got, array)
            step *= ways
        return array

    def exchange(summed):
        return partner(summed) if narrow == 2 else None

    def finish(summed, widths, got=None):
        if narrow == 2:
            got = exchange(summed) if got is None else got
            total = summed.astype(F32) + got.astype(F32)
        else:
            total = lax.psum(summed, "narrow").astype(F32)
        parts = []
        start = 0
        for width in widths:
            parts.append(total[:, start : start + width])
            start += width
        return parts

    def gather_layer(gate_up, down, output, *more):
        if FF // wide == 128:
            packed = down.reshape(8, 16, D // 256, 256).transpose(2, 1, 0, 3).reshape(-1, FF)
            return gather(gate_up, packed, output, *more)
        packed = gather(down).reshape(16, 8, 16, D // 256, 256)
        packed = packed.transpose(0, 3, 2, 1, 4).reshape(D, FF)
        return jnp.concatenate([gather(gate_up), packed, gather(output, *more)], axis=1)

    groups = 8
    group_rows = FF // wide // groups

    def rows_to_down(array):
        cut = array.reshape(-1, D // 256, group_rows, groups, 256)
        return cut.transpose(0, 3, 2, 1, 4).reshape(-1, D)

    def by_pair(array):
        sides = array.shape[1] // D
        return array.reshape(-1, sides, PAIRS, PAIR).swapaxes(1, 2).reshape(array.shape)

    def by_side(array):
        sides = array.shape[1] // D
        return array.reshape(-1, PAIRS, sides, PAIR).swapaxes(1, 2).reshape(array.shape)

    def by_block(array):
        return array.reshape(-1, 2, FF // FF_BLOCK, FF_BLOCK).swapaxes(1, 2).reshape(array.shape)

    def by_half(array):
        return array.reshape(-1, FF // FF_BLOCK, 2, FF_BLOCK).swapaxes(1, 2).reshape(array.shape)

    enc_project, self_project = by_pair(enc_project), by_pair(self_project)
    cross_project = jnp.concatenate([cross_project[:, :D], by_pair(cross_project[:, D:])], axis=1)
    enc_gate_up, dec_gate_up = by_block(enc_gate_up), by_block(dec_gate_up)
    small = jnp.concatenate(
        [norm_gains, header_embed[:, None], jnp.zeros((shard_rows, 121), BF16)], axis=1
    )
    patch_rows_in = take_items(patch_input)
    first_group = gather(enc_project, small)
    second_group = gather_layer(enc_gate_up, enc_down, enc_output, self_project)
    third_group = gather(cross_project[:, D:], cross_project[:, :D], self_output)
    small_all = first_group[:, 3 * D :]
    cross_memory_at = (2 * D, 0)
    cross_query_at = (D, 2 * D)
    self_project_at = (3 * D, 3 * FF + D)
    self_output_at = (D, 3 * D)

    def part_of(array, place):
        return array[:, place[1] : place[1] + place[0]]

    items, patch_rows = patch_rows_in.shape[0], patch_rows_in.shape[1]
    text_rows = text_input.shape[1] * (2 if swapped else 1)
    if swapped:
        patch_total = lax.dynamic_slice_in_dim(patch_count, spot, 1)
        header_total = lax.dynamic_slice_in_dim(header_len, spot, 1)
        text_total = lax.dynamic_slice_in_dim(text_len, spot, 1)
        patch_first = jnp.int32(0)
        text_first = jnp.int32(0)
    else:
        patch_total, header_total, text_total = patch_count, header_len, text_len
        patch_first = spot * patch_rows
        text_first = spot * text_rows
    patch_scalars = jnp.concatenate([patch_first[None], patch_total])
    cross_scalars = jnp.concatenate([text_first[None], patch_total])
    text_scalars = jnp.concatenate([text_first[None], text_total])
    patch_flat = items * patch_rows
    text_flat = items * text_rows

    def all_keys(array):
        return array if swapped else lax.all_gather(array, "narrow", axis=1, tiled=True)

    def own_keys(array):
        if swapped:
            return array
        return lax.psum_scatter(array, "narrow", scatter_dimension=1, tiled=True)

    def split_of(projected):
        if swapped:
            return ((projected, 0), (projected, 1), (projected, 2))
        shape = projected.shape[:2]
        by_pair = projected.reshape(shape + (PAIRS, 3 * PAIR))
        keys = all_keys(by_pair[:, :, :, PAIR:].reshape(shape + (2 * D,)))
        return ((by_pair[:, :, :, :PAIR].reshape(shape + (D,)), 0), (keys, 0), (keys, 1))

    def joined(grads):
        if swapped:
            return grads[0].reshape(-1, grads[0].shape[2])
        query_grad, key_grad = grads[0], own_keys(grads[1])
        pairs = query_grad.shape[2] // PAIR
        shape = query_grad.shape[:2] + (pairs, -1)
        return jnp.concatenate(
            [query_grad.reshape(shape), key_grad.reshape(shape)], axis=3
        ).reshape(-1, 3 * pairs * PAIR)

    gains = small_all[:, :8].astype(F32).T
    header_full = gains[6]

    patch_pos = patch_first + jnp.arange(patch_rows, dtype=jnp.int32)
    header_mask = (
        (patch_pos[None, :] < header_total[:, None]).astype(F32).reshape(patch_flat, 1)
    )
    patch_start = patch_rows_in.astype(F32).reshape(patch_flat, D) + header_mask * header_full
    patch_start, (text_input, patch_cotangent, text_cotangent) = in_order(
        patch_start, (text_input, patch_cotangent, text_cotangent)
    )
    text_rows_in = take_items(text_input)
    patch_grad_in = take_items(patch_cotangent)
    text_grad_in = take_items(text_cotangent)
    attn_input = rms_norm(patch_start, gains[0])
    enc_qkv = (
        matmul(attn_input, first_group[:, : 3 * D])
        .astype(BF16)
        .reshape(items, patch_rows, 3 * D)
    )
    enc_sides = split_of(enc_qkv)
    enc_attended, enc_exact, enc_total = attend_forward(*enc_sides, patch_scalars, False, swapped)
    attn_input, enc_attended = in_order(attn_input, enc_attended)
    attn_turned = turn_rows(attn_input)
    (text_rows_in, patch_grad_in, text_grad_in, attn_turned), enc_attended = in_order(
        (text_rows_in, patch_grad_in, text_grad_in, attn_turned), enc_attended
    )
    enc_attended_flat = enc_attended.reshape(patch_flat, D)
    (
        patch_middle,
        mlp_input,
        enc_slopes,
        enc_hidden,
        patch_rounded,
        patch_final,
        memory_input,
        memory_turned,
    ) = layer_forward(enc_attended_flat, patch_start, second_group, gains, 1, 4)
    memory_input, (cross_output, dec_gate_up, dec_down) = in_order(
        memory_input, (cross_output, dec_gate_up, dec_down)
    )
    fourth_group = gather_layer(dec_gate_up, dec_down, cross_output)
    patch_sent, unused = send_rows(patch_rounded.reshape(items, patch_rows, D))

    text_start = text_rows_in.reshape(text_flat, D)
    self_input = rms_norm(text_start.astype(F32), gains[2])
    self_qkv = (
        matmul(self_input, part_of(second_group, self_project_at))
        .astype(BF16)
        .reshape(items, text_rows, 3 * D)
    )
    self_sides = split_of(self_qkv)
    self_attended, self_exact, self_total = attend_forward(*self_sides, text_scalars, True, swapped)
    self_attended_flat = self_attended.reshape(text_flat, D)
    text_middle = text_start.astype(F32) + matmul(
        self_attended_flat, part_of(third_group, self_output_at)
    )
    cross_input = rms_norm(text_middle, gains[3])
    cross_queries = (
        matmul(cross_input, part_of(third_group, cross_query_at))
        .astype(BF16)
        .reshape(items, text_rows, D)
    )
    memory_kv = all_keys(
        matmul(memory_input, part_of(third_group, cross_memory_at))
        .astype(BF16)
        .reshape(items, patch_rows, 2 * D)
    )
    cross_sides = ((cross_queries, 0), (memory_kv, 0), (memory_kv, 1))
    cross_attended, cross_exact, cross_total = attend_forward(*cross_sides, cross_scalars, False, swapped)
    cross_attended_flat = cross_attended.reshape(text_flat, D)
    patch_sent, cross_attended_flat = in_order(patch_sent, cross_attended_flat)
    text_late, ffn_input, ffn_slopes, ffn_hidden, text_rounded = layer_forward(
        cross_attended_flat, text_middle, fourth_group, gains, 5
    )
    text_sent, unused = send_rows(text_rounded.reshape(items, text_rows, D))

    ffn_out_grad = text_grad_in.reshape(text_flat, D)
    ffn_gate_grad, late_grad, cross_out_grad, cross_head_grad, gain_ffn = layer_backward(
        ffn_out_grad, ffn_slopes, text_late, fourth_group, gains, 5
    )
    cross_head_grad = cross_head_grad.reshape(items, text_rows, D)
    first_width = 2 * FF + FF
    first_terms = fill_weight_grad(None, first_width, 0, ffn_input, ffn_gate_grad, True)
    first_terms = fill_down_grad(
        first_terms, first_width, 2 * FF, shard_rows, ffn_hidden, ffn_out_grad
    )
    first_terms, (cross_out_grad, cross_head_grad) = in_order(
        first_terms, (cross_out_grad, cross_head_grad)
    )
    first_sum = scatter(first_terms)

    second_width = 4 * D
    second_terms = fill_weight_grad(None, second_width, 0, cross_attended_flat, cross_out_grad)
    query_grad, key_grad = attend_backward(
        *cross_sides,
        cross_head_grad,
        cross_exact,
        cross_total,
        cross_scalars,
        False,
        swapped,
    )
    cross_query_grad = query_grad.reshape(text_flat, D)
    memory_kv_grad = own_keys(key_grad).reshape(patch_flat, 2 * D)
    second_terms = fill_weight_grad(second_terms, second_width, D, cross_input, cross_query_grad)
    second_terms = fill_weight_grad(
        second_terms, second_width, 2 * D, memory_turned, memory_kv_grad, True
    )
    second_terms, (cross_query_grad, memory_kv_grad) = in_order(
        second_terms, (cross_query_grad, memory_kv_grad)
    )
    second_sum = scatter(second_terms)
    middle_grad, gain_cross, self_out_grad, self_head_grad = project_back(
        [(cross_query_grad, third_group, cross_query_at)],
        late_grad,
        text_middle,
        gains,
        3,
        True,
        (third_group, self_output_at),
    )
    self_head_grad = self_head_grad.reshape(items, text_rows, D)

    self_terms = fill_weight_grad(None, second_width, 0, self_attended_flat, self_out_grad)
    self_qkv_grad = joined(
        attend_backward(
            *self_sides, self_head_grad, self_exact, self_total, text_scalars, True, swapped
        )
    )
    self_terms = fill_weight_grad(self_terms, second_width, D, self_input, self_qkv_grad)
    (self_terms, first_sum, text_sent), (self_qkv_grad, memory_kv_grad) = in_order(
        (self_terms, first_sum, text_sent), (self_qkv_grad, memory_kv_grad)
    )
    self_sum = scatter(self_terms)

    patch_grad, gain_memory, down_grad = project_back(
        [(memory_kv_grad, third_group, cross_memory_at)],
        patch_grad_in.reshape(patch_flat, D),
        patch_final,
        gains,
        4,
        True,
    )
    enc_gate_grad, enc_middle_grad, enc_out_grad, enc_head_grad, gain_mlp = layer_backward(
        patch_grad, enc_slopes, patch_middle, second_group, gains, 1
    )
    enc_head_grad = enc_head_grad.reshape(items, patch_rows, D)
    third_width = 2 * FF + FF + D
    third_terms = fill_weight_grad(None, third_width, 0, mlp_input, enc_gate_grad, True)
    third_terms = fill_down_grad(
        third_terms, third_width, 2 * FF, shard_rows, enc_hidden, down_grad
    )
    third_terms = fill_weight_grad(
        third_terms, third_width, 3 * FF, enc_attended_flat, enc_out_grad
    )
    (third_terms, second_sum), enc_head_grad = in_order(
        (third_terms, second_sum), enc_head_grad
    )
    third_sum = scatter(third_terms)
    grad_dec_gate_up, grad_dec_down = finish(first_sum, (2 * FF, FF))
    grad_cross_output, grad_cross_query, grad_memory_kv = finish(second_sum, (D, D, 2 * D))
    text_back, gain_self = project_back(
        [(self_qkv_grad, second_group, self_project_at)], middle_grad, text_start, gains, 2
    )
    text_back_sent, unused = send_rows(text_back.reshape(items, text_rows, D))

    enc_qkv_grad = joined(
        attend_backward(
            *enc_sides, enc_head_grad, enc_exact, enc_total, patch_scalars, False, swapped
        )
    )
    late = (
        text_back_sent,
        gain_self,
        self_sum,
        third_sum,
        grad_dec_gate_up,
        grad_dec_down,
        grad_cross_output,
        grad_cross_query,
        grad_memory_kv,
    )
    late, enc_qkv_grad = in_order(late, enc_qkv_grad)
    (
        text_back_sent,
        gain_self,
        self_sum,
        third_sum,
        grad_dec_gate_up,
        grad_dec_down,
        grad_cross_output,
        grad_cross_query,
        grad_memory_kv,
    ) = late
    fourth_terms = fill_weight_grad(
        None, 3 * D, 0, attn_turned, enc_qkv_grad, True
    )
    fourth_terms, enc_qkv_grad = in_order(fourth_terms, enc_qkv_grad)
    fourth_sum = scatter(fourth_terms)
    self_got, third_got = exchange(self_sum), exchange(third_sum)

    start_grad, gain_attn = project_back(
        [(enc_qkv_grad, first_group, (3 * D, 0))], enc_middle_grad, patch_start, gains, 0
    )
    floating = (self_got, third_got, patch_sent, text_sent, text_back_sent)
    floating, start_grad = in_order(floating, start_grad)
    self_got, third_got, patch_sent, text_sent, text_back_sent = floating
    patch_back_sent, start_grad = send_rows(
        start_grad.reshape(items, patch_rows, D), start_grad
    )
    header_term = jnp.sum(start_grad * header_mask, axis=0, keepdims=True)
    terms = (gain_attn, gain_mlp, gain_self, gain_cross, gain_memory, gain_ffn, header_term)
    small_term = jnp.concatenate([term[:1] for term in terms + (jnp.zeros_like(header_term),)])
    small_own = lax.dynamic_slice_in_dim(
        sum_small(small_term), lax.axis_index("wide") * shard_rows, shard_rows, 1
    ).T
    (grad_small,) = finish(small_own.astype(BF16), (small_own.shape[1],))

    grad_self_output, grad_self_project = finish(self_sum, (D, 3 * D), self_got)
    grad_enc_gate_up, grad_enc_down, grad_enc_output = finish(
        third_sum, (2 * FF, FF, D), third_got
    )
    (grad_enc_project,) = finish(fourth_sum, (3 * D,))
    patch_output = place_rows(patch_sent)
    text_output = place_rows(text_sent)
    text_input_grad = place_rows(text_back_sent)
    if swapped:
        patch_input_grad = place_halves(spot, start_grad, patch_back_sent[1])
    else:
        patch_input_grad = patch_back_sent[0]
    grad_cross_project = jnp.concatenate([grad_cross_query, by_side(grad_memory_kv)], axis=1)
    return (
        patch_output,
        text_output,
        patch_input_grad,
        text_input_grad,
        grad_small[:, :6],
        grad_small[:, 6],
        by_side(grad_enc_project),
        grad_enc_output,
        by_half(grad_enc_gate_up),
        rows_to_down(grad_enc_down),
        by_side(grad_self_project),
        grad_self_output,
        grad_cross_project,
        grad_cross_output,
        by_half(grad_dec_gate_up),
        rows_to_down(grad_dec_down),
    )


def solution(mesh):
    rows = P("wide", "narrow", None)
    weight = P("wide", None)
    vector = P("wide")
    return jax.shard_map(
        functools.partial(on_device, mesh.shape["narrow"]),
        mesh=mesh,
        in_specs=(rows,) * 4 + (vector,) * 3 + (weight, vector) + (weight,) * 10,
        out_specs=(rows,) * 4 + (weight, vector) + (weight,) * 10,
        check_vma=False,
    )
```
